128 devices in a mesh: shard: 8 (over z, core), replica: 16 (over y, x).
Axes of the slice: x: 4, y: 4, z: 4, core: 2. Of those that a mesh axis runs over, the one named last changes fastest.
Arguments:
- partial_grads: bfloat16 [16, 128, 512, 512], P('replica', 'shard'), may hold values from -64 to 64
- owner_list: int32 [128, 1], replicated, may hold values from 0 to 15; in each aligned block of 16 rows (0 to 15, 16 to 31, ...) at most 2 rows name the same one
- left_stat: float32 [8, 16, 2, 512, 512], P('shard', 'replica'), may hold values from -1 to 5, as said below
- right_stat: float32 [8, 16, 2, 512, 512], P('shard', 'replica'), may hold values from -1 to 5, as said below
- left_root: float32 [8, 16, 2, 512, 512], P('shard', 'replica'), may hold values from -1 to 2, as said below
- right_root: float32 [8, 16, 2, 512, 512], P('shard', 'replica'), may hold values from -1 to 2, as said below
Outputs:
- update: bfloat16 [128, 512, 512], P(('shard', 'replica'))
- left_new: float32 [8, 16, 2, 512, 512], P('shard', 'replica')
- right_new: float32 [8, 16, 2, 512, 512], P('shard', 'replica')
The draws below stay inside these ranges and needn't reach their ends.
Inputs may be any that keep to these rules, and one draw needn't show every extreme that they name: `owner_list`: among the 16 blocks of one column no owner is named more than 2 times, a bound that some block reaches. `left_stat`: Symmetric. `right_stat`: Symmetric. `left_root`: Symmetric. `right_root`: Symmetric.
All inputs are finite; a program needn't handle non-finite values.
Results may differ from the reference program's by a relative error of at most 0.02.
Values may be sent and summed in bfloat16 or wider, within the bound.
A program may use at most 128 MiB of HBM per device.

```python
import math
import jax
import jax.numpy as jnp
import numpy as np
from jax import lax

B = 512
SLOTS = 2
BLOCKS = 128
N_SHARD = 8
N_REPLICA = 16


half_root = 0.70710678


def log_uniform(key, dims, low_end, high_end):
    return jnp.exp(jax.random.uniform(key, dims, jnp.float32, jnp.log(low_end), jnp.log(high_end)))


def symmetric(key, jitter, low_end, high_end):
    dims = jitter.shape
    diagonal = log_uniform(key, dims[:-1], low_end, high_end)
    row_idx = lax.broadcasted_iota(jnp.int32, (dims[-1], dims[-1]), 0)
    col_idx = lax.broadcasted_iota(jnp.int32, (dims[-1], dims[-1]), 1)
    on_diag = row_idx == col_idx
    off_diag = (jitter + jnp.swapaxes(jitter, -1, -2)) * half_root
    return jnp.where(on_diag, diagonal[..., None, :], off_diag)


def draw_partial_grads(key, part):
    key = jax.random.fold_in(key, 11)
    dims = (N_REPLICA, BLOCKS, B, B)
    row_scale = log_uniform(jax.random.fold_in(key, 1), (BLOCKS, B, 1), 0.3, 3.0)
    col_scale = log_uniform(jax.random.fold_in(key, 2), (BLOCKS, 1, B), 0.3, 3.0)
    block_place = jnp.arange(BLOCKS, dtype=jnp.float32).reshape(BLOCKS, 1, 1) / max(BLOCKS - 1, 1)
    jitter = jnp.clip(jax.random.normal(jax.random.fold_in(key, 3), dims, jnp.float32), -4.0, 4.0)
    block_ramp = 1.0 + 2.0 * block_place
    return (0.25 * jitter * row_scale * col_scale * block_ramp).astype(jnp.bfloat16)


def stat_jitter(key):
    dims = (N_SHARD, N_REPLICA, SLOTS, B, B)
    return 0.2 * jnp.clip(jax.random.normal(key, dims, jnp.float32), -2.5, 2.5)


def root_jitter(key):
    dims = (N_SHARD, N_REPLICA, SLOTS, B, B)
    spread = 0.6 / B ** 0.5
    return spread * jnp.clip(jax.random.normal(key, dims, jnp.float32), -3.0, 3.0)


def draw_left_stat(key, part):
    key = jax.random.fold_in(key, 21)
    return symmetric(jax.random.fold_in(key, 1), stat_jitter(jax.random.fold_in(key, 2)), 0.5, 5.0)


def draw_right_stat(key, part):
    key = jax.random.fold_in(key, 31)
    return symmetric(jax.random.fold_in(key, 1), stat_jitter(jax.random.fold_in(key, 2)), 0.5, 5.0)


def draw_left_root(key, part):
    key = jax.random.fold_in(key, 41)
    return symmetric(jax.random.fold_in(key, 1), root_jitter(jax.random.fold_in(key, 2)), 0.5, 2.0)


def draw_right_root(key, part):
    key = jax.random.fold_in(key, 51)
    return symmetric(jax.random.fold_in(key, 1), root_jitter(jax.random.fold_in(key, 2)), 0.5, 2.0)


def routed_block(own_key, own, number, rows, amount, top, most, lean):
    order = jax.random.permutation(own_key, amount)
    heavy_load, ordinary = load_shares(amount, rows * top, most, lean, True), load_shares(amount, rows * top, most, lean, False)
    places = jnp.arange(amount)

    def named(tallies, rotation):
        used = int((tallies > 0).sum())
        fixed = max(1, used // 4)
        shifted = fixed + (places - fixed + rotation * (used - fixed)) % max(1, amount - fixed)
        return jnp.zeros((amount,), jnp.int32).at[order[jnp.where(places < fixed, places, shifted)]].set(jnp.asarray(tallies, jnp.int32))

    tallies = jnp.where(number % 4 == 0, named(heavy_load, number // 4), named(ordinary, number - number // 4 - 1))
    mixed = jax.random.permutation(jax.random.fold_in(own, 3), amount)
    giver, sink = mixed[0:amount // 2 * 2:2], mixed[1:amount // 2 * 2:2]
    slack = jnp.minimum(tallies[giver] - 1, most - tallies[sink]) // 2
    slack = jnp.where((giver == order[0]) | (sink == order[0]) | (tallies[sink] == 0), 0, jnp.maximum(slack, 0))
    shifted = jax.random.randint(jax.random.fold_in(own, 4), (amount // 2,), 0, 1 << 20) % (slack + 1)
    tallies = tallies.at[giver].add(-shifted).at[sink].add(shifted)
    labels = jnp.searchsorted(jnp.cumsum(tallies), jnp.arange(rows * top), side="right").astype(jnp.int32)
    listing = labels.reshape(top, rows).T
    listing = listing[jax.random.permutation(jax.random.fold_in(own, 1), rows)]
    rotation = jax.random.randint(jax.random.fold_in(own, 2), (rows, 1), 0, top)
    return jnp.take_along_axis(listing, (jnp.arange(top)[None, :] + rotation) % top, axis=1)


def load_shares(count, total, limit, skew, full):
    loads = [(1 << 20) // math.isqrt(grade ** skew) + 1 for grade in range(1, count + 1)]
    largest = limit if full else min(limit, max(-(-total // count), total * loads[0] // sum(loads)))
    least = 1 if total - largest >= count - 1 else 0
    given, surplus = [largest] + [least] * (count - 1), total - largest - least * (count - 1)
    while surplus > 0:
        movable = [i for i in range(1, count) if given[i] < largest] or [i for i in range(1, count) if given[i] < limit]
        pool, remaining = sum([loads[i] for i in movable]), surplus
        for i in movable:
            more = min(limit - given[i], max(1, remaining * loads[i] // pool), surplus)
            given[i] = given[i] + more
            surplus = surplus - more
    return np.array(given)


def setup_inputs(seed: int = 0) -> dict:
    splits = jax.random.split(jax.random.key(seed), 7)
    partial_grads = draw_partial_grads(jax.random.fold_in(splits[6], 71), 0)
    owner_list_keys = jax.random.split(jax.random.fold_in(splits[1], 1), BLOCKS // N_REPLICA)
    owner_list_turns = jax.random.permutation(jax.random.fold_in(splits[1], 3), BLOCKS // N_REPLICA)
    owner_list = jax.vmap(lambda own, number: routed_block(jax.random.fold_in(splits[1], 2), own, number, N_REPLICA, N_REPLICA, 1, SLOTS, 2))(owner_list_keys, owner_list_turns).reshape((BLOCKS, 1))
    left_stat = draw_left_stat(jax.random.fold_in(splits[6], 71), 0)
    right_stat = draw_right_stat(jax.random.fold_in(splits[6], 71), 0)
    left_root = draw_left_root(jax.random.fold_in(splits[6], 71), 0)
    right_root = draw_right_root(jax.random.fold_in(splits[6], 71), 0)
    return dict(partial_grads=partial_grads, owner_list=owner_list, left_stat=left_stat, right_stat=right_stat, left_root=left_root, right_root=right_root)


decay_keep = 0.9
epsilon = 1e-06
rms_limit = 0.5

def slot_table(owner_list):
    owners = owner_list[:, 0].astype(jnp.int32).reshape(N_SHARD, N_REPLICA)
    position = jnp.arange(N_REPLICA, dtype=jnp.int32)
    same_owner = owners[:, :, None] == owners[:, None, :]
    earlier = position[None, :] < position[:, None]
    slot_index = lax.optimization_barrier(jnp.sum((same_owner & earlier[None]).astype(jnp.int32), axis=2))
    return (owners.reshape(-1), slot_index.reshape(-1).astype(jnp.int32))

def reference(partial_grads, owner_list, left_stat, right_stat, left_root, right_root):
    owner_ids, slot_ids = slot_table(owner_list)
    col_ids = (jnp.arange(BLOCKS, dtype=jnp.int32) // N_REPLICA).astype(jnp.int32)

    def one_block(block_id):
        col_id = col_ids[block_id]
        owner_id = owner_ids[block_id]
        slot_id = slot_ids[block_id]
        replica_terms = lax.dynamic_index_in_dim(partial_grads, block_id, 1, keepdims=False)
        gradient = lax.optimization_barrier(jnp.sum(replica_terms.astype(jnp.float32), axis=0)).astype(jnp.bfloat16)
        left_old = left_stat[col_id, owner_id, slot_id]
        right_old = right_stat[col_id, owner_id, slot_id]
        left_fresh = decay_keep * left_old + (1.0 - decay_keep) / B * jnp.dot(gradient, gradient.T, preferred_element_type=jnp.float32)
        right_fresh = decay_keep * right_old + (1.0 - decay_keep) / B * jnp.dot(gradient.T, gradient, preferred_element_type=jnp.float32)
        grad_wide = gradient.astype(jnp.float32)
        precond = jnp.dot(left_root[col_id, owner_id, slot_id], grad_wide, precision=lax.Precision.HIGHEST)
        precond = jnp.dot(precond, right_root[col_id, owner_id, slot_id], precision=lax.Precision.HIGHEST)
        graft = jnp.sqrt(jnp.mean(grad_wide * grad_wide) + epsilon) / jnp.sqrt(jnp.mean(precond * precond) + epsilon)
        return (left_fresh, right_fresh, precond * graft, jnp.sum(grad_wide * grad_wide))
    lefts, rights, scaled, squares = lax.map(one_block, jnp.arange(BLOCKS, dtype=jnp.int32))
    grad_rms = jnp.sqrt(jnp.sum(squares) / (BLOCKS * B * B))
    clip_scale = jnp.minimum(1.0, rms_limit / grad_rms)
    update = (scaled * clip_scale).astype(jnp.bfloat16)
    left_new = left_stat.at[col_ids, owner_ids, slot_ids].set(lefts)
    right_new = right_stat.at[col_ids, owner_ids, slot_ids].set(rights)
    return (update, left_new, right_new)
```

```python
import functools

import jax
import jax.numpy as jnp
from jax import lax
from jax.experimental import pallas as pl
from jax.experimental.pallas import tpu as pltpu
from jax.sharding import PartitionSpec as P

decay_keep = 0.9
epsilon = 1e-06
rms_limit = 0.5

MESH = pl.DeviceIdType.MESH
f32 = jnp.float32
bf16 = jnp.bfloat16

SIDE = 4
REPS = 16
COLS = 8
SLOTS = 2
BLOCK = 512
PIECE = 32
HALF = 16
WIDE = 256
STEPS = BLOCK // WIDE


def kernel(
    grads, owners, left_stat, right_stat, left_root, right_root,
    update, left_out, right_out,
    far_in, near_in, both_in, near_own, last_own, line_sum, line_in, piece,
    to_owner, block_in, root_in, root_hi, root_lo, stat_in, precond, ready,
    held_first, held_last, to_place, squares, squares_in, table,
    load_sem, root_sem, stat_sem, out_sem, own_sem,
    far_s, far_r, near_s, near_r, both_s, both_r, line_s, line_r,
    owner_s, owner_r, held_s, held_r, place_s, place_r,
    zsum_s, zsum_r, psum_s, psum_r,
):
    s = lax.axis_index("shard")
    r = lax.axis_index("replica")
    x, y = r % SIDE, r // SIDE

    def along(half, step):
        if half == 0:
            return (s, y * SIDE + (x + step) % SIDE)
        return (s, (y + step) % SIDE * SIDE + x)

    def send(src, dst, send_sem, recv_sem, device):
        return pltpu.make_async_remote_copy(
            src_ref=src, dst_ref=dst, send_sem=send_sem, recv_sem=recv_sem,
            device_id=device, device_id_type=MESH,
        )

    def chunk(half, step, first, count, wide):
        place = ((x if half == 0 else y) + step) % SIDE
        rows = pl.ds(first, count)
        cols = pl.ds(wide * WIDE, WIDE)
        if half == 0:
            return grads.at[rows, :, place, 0, :, cols]
        return grads.at[rows, place, :, 1, :, cols]

    barrier = pltpu.get_barrier_semaphore()

    @pl.loop(1, REPS)
    def _(d):
        pl.semaphore_signal(barrier, inc=1, device_id=(s, (r + d) % REPS), device_id_type=MESH)

    @pl.loop(1, COLS)
    def _(d):
        pl.semaphore_signal(barrier, inc=1, device_id=((s + d) % COLS, r), device_id_type=MESH)

    pl.semaphore_wait(barrier, REPS + COLS - 2)

    held = (held_first, held_last)
    groups = [(wide, half) for wide in range(STEPS) for half in range(2)]

    def far(g, way):
        wide, half = groups[g]
        return send(chunk(half, 2, 8 * way, 8, wide), far_in.at[g, way],
                    far_s.at[g, way], far_r.at[g, way], along(half, 1 - 2 * way))

    def near(g, way):
        wide, half = groups[g]
        return send(chunk(half, 1 - 2 * way, 8 - 8 * way, 8, wide), near_in.at[g, way],
                    near_s.at[g, way], near_r.at[g, way], along(half, 1 - 2 * way))

    def both(g, way):
        wide, half = groups[g]
        return send(near_own.at[g, way], both_in.at[g, way],
                    both_s.at[g, way], both_r.at[g, way], along(half, 1 - 2 * way))

    def line(g, d):
        wide, half = groups[g]
        place = ((y if half == 0 else x) + d) % SIDE
        return send(line_sum.at[g, place], line_in.at[g, d - 1],
                    line_s.at[g, d - 1], line_r.at[g, d - 1], along(1 - half, d))

    def load_near(g, way):
        wide, half = groups[g]
        return pltpu.make_async_copy(chunk(half, 1 - 2 * way, 8 * way, 8, wide),
                                     near_own.at[g, way], load_sem.at[g, way])

    def load_last(g):
        wide, half = groups[g]
        return pltpu.make_async_copy(chunk(half, 0, 0, REPS, wide),
                                     last_own.at[g], load_sem.at[g, 2])

    for g in range(len(groups)):
        for way in range(2):
            far(g, way).start()
            load_near(g, way).start()
        load_last(g).start()
        for way in range(2):
            near(g, way).start()

    roots = [pltpu.make_async_copy(ref, root_in.at[i], root_sem.at[i])
             for i, ref in enumerate((left_root, right_root))]
    stats = [pltpu.make_async_copy(ref, stat_in.at[i], stat_sem.at[i])
             for i, ref in enumerate((left_stat, right_stat))]
    for copy in roots + stats:
        copy.start()

    @pl.loop(0, REPS)
    def _(j):
        mine = owners[0, s * REPS + j]
        count = jnp.int32(0)
        for i in range(REPS):
            hit = (owners[0, s * REPS + i] == mine) & (i < j)
            count = count + hit.astype(jnp.int32)
        table[1, j] = mine
        table[2, j] = jnp.minimum(count, SLOTS - 1)

    @pl.loop(0, REPS)
    def _(o):
        first, second = jnp.int32(REPS), jnp.int32(REPS)
        for j in range(REPS):
            hit = table[1, j] == o
            first = jnp.where(hit & (table[2, j] == 0), j, first)
            second = jnp.where(hit & (table[2, j] == 1), j, second)
        table[0, o * SLOTS] = first
        table[0, o * SLOTS + 1] = second

    for wide in range(STEPS):
        piece[wide, REPS] = jnp.zeros((PIECE, WIDE), bf16)

    for copy in roots:
        copy.wait()

    @pl.loop(0, 2 * SLOTS * 8)
    def _(i):
        side, k, t = i // (SLOTS * 8), i // 8 % SLOTS, i % 8
        rows = pl.ds(pl.multiple_of(t * 64, 64), 64)
        whole = root_in[side, k, rows, :]
        top = whole.astype(bf16)
        root_hi[side, k, rows, :] = top
        root_lo[side, k, rows, :] = (whole - top.astype(f32)).astype(bf16)

    squares[...] = jnp.zeros_like(squares)

    def combine(g):
        for way in range(2):
            load_near(g, way).wait()
            far(g, way).wait_recv()

            @pl.loop(0, 8)
            def _(b):
                near_own[g, way, b] = near_own[g, way, b] + far_in[g, way, b]

            both(g, way).start()

    def line_total(g):
        load_last(g).wait()
        for way in range(2):
            near(g, way).wait_recv()
            both(g, way).wait_recv()

        @pl.loop(0, 8)
        def _(b):
            for way in range(2):
                total = (last_own[g, 8 * way + b].astype(f32)
                         + both_in[g, way, b].astype(f32)
                         + near_in[g, 1 - way, b].astype(f32))
                line_sum[g, :, 8 * way + b] = total.astype(bf16)

        for d in (2, 1, 3):
            line(g, d).start()

    def total(g):
        wide, half = groups[g]
        for d in (1, 2, 3):
            line(g, d).wait_recv()
        place = y if half == 0 else x

        @pl.loop(0, REPS)
        def _(b):
            value = line_sum[g, place, b].astype(f32)
            for d in range(3):
                value = value + line_in[g, d, b].astype(f32)
            value = value.astype(bf16)
            piece[wide, b, pl.ds(half * HALF, HALF), :] = value
            value = value.astype(f32)
            value = value * value
            value = value[:, :128] + value[:, 128:]
            squares[0] += value[:8] + value[8:]

    def owner(wide, d):
        return send(to_owner.at[wide, (r + d) % REPS], block_in.at[wide, :, r],
                    owner_s.at[wide, d], owner_r.at[wide, d], (s, (r + d) % REPS))

    def route(wide):
        @pl.loop(0, REPS)
        def _(o):
            for k in range(SLOTS):
                to_owner[wide, o, k] = piece[wide, table[0, o * SLOTS + k]]

        @pl.loop(1, REPS)
        def _(d):
            owner(wide, d).start()

        block_in[wide, :, r] = to_owner[wide, r]

    def wait_route(wide):
        @pl.loop(1, REPS)
        def _(d):
            owner(wide, d).wait_recv()

    def product(wide):
        @pl.loop(0, SLOTS * 2)
        def _(i):
            k, t = i // 2, i % 2
            rows = pl.ds(pl.multiple_of(t * 256, 256), 256)
            block = block_in[wide, k].reshape(BLOCK, WIDE)
            part = (jnp.dot(root_hi[0, k, rows, :], block, preferred_element_type=f32)
                    + jnp.dot(root_lo[0, k, rows, :], block, preferred_element_type=f32))
            top = part.astype(bf16)
            low = (part - top.astype(f32)).astype(bf16)
            across = pl.ds(wide * WIDE, WIDE)
            hi, lo = root_hi[1, k, across, :], root_lo[1, k, across, :]
            value = (jnp.dot(top, hi, preferred_element_type=f32)
                     + jnp.dot(top, lo, preferred_element_type=f32)
                     + jnp.dot(low, hi, preferred_element_type=f32))
            if wide == 0:
                precond[k, rows, :] = value
            else:
                precond[k, rows, :] += value

    combine(0)
    combine(1)
    combine(2)
    combine(3)
    line_total(0)
    line_total(1)
    total(0)
    total(1)
    route(0)
    line_total(2)
    line_total(3)
    total(2)
    total(3)
    route(1)

    def zsum(d):
        return send(squares.at[0], squares_in.at[d], zsum_s.at[d], zsum_r.at[d], ((s + d) % COLS, r))

    def psum(d):
        return send(squares.at[1], squares_in.at[COLS + d], psum_s.at[d], psum_r.at[d], (s, (r + d) % REPS))

    for d in range(1, COLS):
        zsum(d).start()

    wait_route(0)
    product(0)

    column = squares[0]
    for d in range(1, COLS):
        zsum(d).wait_recv()
        column = column + squares_in[d]
    squares[1] = column

    @pl.loop(1, REPS)
    def _(d):
        psum(d).start()

    wait_route(1)
    product(1)

    def hold(wide, d):
        return send(ready.at[wide, :, (r + d) % REPS], held[wide].at[r],
                    held_s.at[wide, d], held_r.at[wide, d], (s, (r + d) % REPS))

    scales = []
    for k in range(SLOTS):
        def square_sum(i, carry):
            value, power = carry
            across = pl.ds(pl.multiple_of(i * PIECE, PIECE), PIECE)
            p = precond[k, across, :]
            power = power + p * p
            for wide in range(STEPS):
                g = block_in[wide, k, i].astype(f32)
                value = value + g * g
            return value, power

        value, power = lax.fori_loop(
            0, REPS, square_sum, (jnp.zeros((PIECE, WIDE), f32), jnp.zeros((PIECE, BLOCK), f32)))
        value = jnp.sum(value, axis=(0, 1), keepdims=True) / (BLOCK * BLOCK)
        power = jnp.sum(power, axis=(0, 1), keepdims=True) / (BLOCK * BLOCK)
        scales.append(jnp.sqrt(value + epsilon) / jnp.sqrt(power + epsilon))

    all_squares = squares[1]
    for d in range(1, REPS):
        psum(d).wait_recv()
        all_squares = all_squares + squares_in[COLS + d]
    rms = jnp.sqrt(jnp.sum(all_squares, axis=(0, 1), keepdims=True)
                   / (COLS * REPS * BLOCK * BLOCK))
    clip = jnp.minimum(1.0, rms_limit / rms)

    scales = [scale * clip for scale in scales]

    for wide in range(STEPS):
        for k in range(SLOTS):
            @pl.loop(0, REPS)
            def _(i):
                across = pl.ds(pl.multiple_of(i * PIECE, PIECE), PIECE)
                value = precond[k, across, pl.ds(wide * WIDE, WIDE)] * scales[k]
                ready[wide, k, i] = value.astype(bf16)

        @pl.loop(1, REPS)
        def _(d):
            hold(wide, d).start()

        held[wide][r] = ready[wide, :, r]

    for copy in stats:
        copy.wait()

    @pl.loop(0, SLOTS)
    def _(k):
        filled = table[0, r * SLOTS + k] < REPS
        keep = jnp.where(filled, decay_keep, 1.0).astype(f32)
        weight = (1.0 - decay_keep) / BLOCK
        for t in range(2):
            rows = pl.ds(t * 256, 256)
            left = jnp.zeros((256, BLOCK), f32)
            for wide in range(STEPS):
                block = block_in[wide, k].reshape(BLOCK, WIDE)
                left = left + lax.dot_general(
                    block[t * 256:(t + 1) * 256], block, (((1,), (1,)), ((), ())),
                    preferred_element_type=f32)
            stat_in[0, k, rows, :] = keep * stat_in[0, k, rows, :] + weight * left
            for wide in range(STEPS):
                across = pl.ds(wide * WIDE, WIDE)
                right = lax.dot_general(
                    block_in[t, k].reshape(BLOCK, WIDE), block_in[wide, k].reshape(BLOCK, WIDE),
                    (((0,), (0,)), ((), ())), preferred_element_type=f32)
                stat_in[1, k, rows, across] = keep * stat_in[1, k, rows, across] + weight * right

    outs = [pltpu.make_async_copy(stat_in.at[i], ref, out_sem.at[i])
            for i, ref in enumerate((left_out, right_out))]
    for copy in outs:
        copy.start()

    def settle(wide, d):
        return send(to_place.at[wide, (r + d) % REPS], update.at[r, :, pl.ds(wide * WIDE, WIDE)],
                    place_s.at[wide, d], place_r.at[wide, d], (s, (r + d) % REPS))

    own = []
    for wide in range(STEPS):
        @pl.loop(1, REPS)
        def _(d):
            hold(wide, d).wait_recv()

        @pl.loop(0, REPS)
        def _(j):
            to_place[wide, j] = held[wide][table[1, j], table[2, j]]

        @pl.loop(1, REPS)
        def _(d):
            settle(wide, d).start()

        own.append(pltpu.make_async_copy(
            to_place.at[wide, r], update.at[r, :, pl.ds(wide * WIDE, WIDE)], own_sem.at[wide]))
        own[-1].start()

    for g in range(len(groups)):
        for way in range(2):
            far(g, way).wait_send()
            near(g, way).wait_send()
            both(g, way).wait_send()
        for d in (1, 2, 3):
            line(g, d).wait_send()
    for d in range(1, COLS):
        zsum(d).wait_send()
    for copy in outs + own:
        copy.wait()

    @pl.loop(1, REPS)
    def _(d):
        psum(d).wait_send()
        for wide in range(STEPS):
            owner(wide, d).wait_send()
            hold(wide, d).wait_send()
            settle(wide, d).wait_send()
            settle(wide, d).wait_recv()


def on_device(partial_grads, owner_list, left_stat, right_stat, left_root, right_root):
    grads = partial_grads.reshape(REPS, SIDE, SIDE, 2, HALF, BLOCK)
    any_spec = pl.BlockSpec(memory_space=pl.ANY)
    dma = pltpu.SemaphoreType.DMA
    groups = 2 * STEPS
    pair = [dma((groups, 2))] * 2
    ring = [dma((STEPS, REPS))] * 2
    state = jax.ShapeDtypeStruct((SLOTS, BLOCK, BLOCK), f32)
    update, left_new, right_new = pl.pallas_call(
        kernel,
        out_shape=(
            jax.ShapeDtypeStruct((REPS, PIECE, BLOCK), bf16),
            state,
            state,
        ),
        in_specs=[any_spec, pl.BlockSpec(memory_space=pltpu.SMEM)] + [any_spec] * 4,
        out_specs=(any_spec, any_spec, any_spec),
        scratch_shapes=[
            pltpu.VMEM((groups, 2, 8, SIDE, HALF, WIDE), bf16),
            pltpu.VMEM((groups, 2, 8, SIDE, HALF, WIDE), bf16),
            pltpu.VMEM((groups, 2, 8, SIDE, HALF, WIDE), bf16),
            pltpu.VMEM((groups, 2, 8, SIDE, HALF, WIDE), bf16),
            pltpu.VMEM((groups, REPS, SIDE, HALF, WIDE), bf16),
            pltpu.VMEM((groups, SIDE, REPS, HALF, WIDE), bf16),
            pltpu.VMEM((groups, 3, REPS, HALF, WIDE), bf16),
            pltpu.VMEM((STEPS, REPS + 1, PIECE, WIDE), bf16),
            pltpu.VMEM((STEPS, REPS, SLOTS, PIECE, WIDE), bf16),
            pltpu.VMEM((STEPS, SLOTS, REPS, PIECE, WIDE), bf16),
            pltpu.VMEM((2, SLOTS, BLOCK, BLOCK), f32),
            pltpu.VMEM((2, SLOTS, BLOCK, BLOCK), bf16),
            pltpu.VMEM((2, SLOTS, BLOCK, BLOCK), bf16),
            pltpu.VMEM((2, SLOTS, BLOCK, BLOCK), f32),
            pltpu.VMEM((SLOTS, BLOCK, BLOCK), f32),
            pltpu.VMEM((STEPS, SLOTS, REPS, PIECE, WIDE), bf16),
            pltpu.VMEM((REPS, SLOTS, PIECE, WIDE), bf16),
            pltpu.VMEM((REPS, SLOTS, PIECE, WIDE), bf16),
            pltpu.VMEM((STEPS, REPS, PIECE, WIDE), bf16),
            pltpu.VMEM((2, 8, 128), f32),
            pltpu.VMEM((COLS + REPS, 8, 128), f32),
            pltpu.SMEM((3, REPS * SLOTS), jnp.int32),
            dma((groups, 3)), dma((2,)), dma((2,)), dma((2,)), dma((STEPS,)),
        ] + pair + pair + pair + [dma((groups, 3))] * 2 + ring + ring + ring
        + [dma((COLS,))] * 2 + [dma((REPS,))] * 2,
        compiler_params=pltpu.CompilerParams(
            collective_id=0, has_side_effects=True, vmem_limit_bytes=58 << 20),
    )(grads, owner_list.reshape(1, COLS * REPS), left_stat[0, 0], right_stat[0, 0], left_root[0, 0], right_root[0, 0])
    return (update.reshape(1, BLOCK, BLOCK), left_new[None, None], right_new[None, None])


def solution(mesh):
    return jax.shard_map(
        on_device,
        mesh=mesh,
        in_specs=(
            P("replica", "shard", None, None),
            P(),
            P("shard", "replica", None, None, None),
            P("shard", "replica", None, None, None),
            P("shard", "replica", None, None, None),
            P("shard", "replica", None, None, None),
        ),
        out_specs=(
            P(("shard", "replica"), None, None),
            P("shard", "replica", None, None, None),
            P("shard", "replica", None, None, None),
        ),
        check_vma=False,
    )
```

```python
import functools

import jax
import jax.numpy as jnp
from jax import lax
from jax.experimental import pallas as pl
from jax.experimental.pallas import tpu as pltpu
from jax.sharding import PartitionSpec as P

decay_keep = 0.9
epsilon = 1e-06
rms_limit = 0.5

MESH = pl.DeviceIdType.MESH
f32 = jnp.float32
bf16 = jnp.bfloat16

SIDE = 4
REPS = 16
COLS = 8
ROOT = 1
SLOTS = 2
BLOCK = 512
PIECE = 32
HALF = 16
WIDE = 128
STEPS = BLOCK // WIDE
BACK = 256
TURNS = BLOCK // BACK


def kernel(
    grads, owner_list, left_stat, right_stat, left_root, right_root,
    update, left_out, right_out,
    far_in, near_in, both_in, near_own, last_own,
    line_sum, line_far, line_near, line_both, line_in, piece,
    to_owner, block_in, root_in, root_hi, root_lo, stat_in, precond, ready,
    held_first, held_last, scale_own, scale_in, to_place,
    squares, squares_in, column, column_in, owners, table,
    load_sem, root_sem, stat_sem, list_sem,
    far_s, far_r, near_s, near_r, both_s, both_r,
    lfar_s, lfar_r, lnear_s, lnear_r, lboth_s, lboth_r, line_s, line_r,
    owner_s, owner_r, held_s, held_r, scale_s, scale_r, place_s, place_r,
    square_s, square_r, column_s, column_r,
):
    s = lax.axis_index("shard")
    r = lax.axis_index("replica")
    x, y = r % SIDE, r // SIDE
    held = (held_first, held_last)

    def along(half, step):
        if half == 0:
            return (s, y * SIDE + (x + step) % SIDE)
        return (s, (y + step) % SIDE * SIDE + x)

    def other(d):
        return (s, (r + d) % REPS)

    def send(src, dst, send_sem, recv_sem, device):
        return pltpu.make_async_remote_copy(
            src_ref=src, dst_ref=dst, send_sem=send_sem, recv_sem=recv_sem,
            device_id=device, device_id_type=MESH,
        )

    barrier = pltpu.get_barrier_semaphore()
    for half in range(2):
        for step in (1, 3):
            pl.semaphore_signal(barrier, inc=1, device_id=along(half, step), device_id_type=MESH)

    @pl.when(s == ROOT)
    def _():
        @pl.loop(1, COLS)
        def _(d):
            pl.semaphore_signal(barrier, inc=1, device_id=((s + d) % COLS, r), device_id_type=MESH)

        pl.semaphore_wait(barrier, 4)

    @pl.when(s != ROOT)
    def _():
        pl.semaphore_wait(barrier, 5)

    def chunk(g, step, first, count):
        wide, half = g // 2, g % 2
        place = ((x if half == 0 else y) + step) % SIDE
        rows = pl.ds(first, count)
        cols = pl.ds(wide * WIDE, WIDE)
        if half == 0:
            return grads.at[rows, :, place, 0, :, cols]
        return grads.at[rows, place, :, 1, :, cols]

    def far(g, way):
        return send(chunk(g, 2, 8 * way, 8), far_in.at[g, way],
                    far_s.at[g, way], far_r.at[g, way], along(g % 2, 1 - 2 * way))

    def near(g, way):
        return send(chunk(g, 1 - 2 * way, 8 - 8 * way, 8), near_in.at[g, way],
                    near_s.at[g, way], near_r.at[g, way], along(g % 2, 1 - 2 * way))

    def both(g, way):
        return send(near_own.at[g, way], both_in.at[g, way],
                    both_s.at[g, way], both_r.at[g, way], along(g % 2, 1 - 2 * way))

    def load_near(g, way):
        return pltpu.make_async_copy(chunk(g, 1 - 2 * way, 8 * way, 8),
                                     near_own.at[g, way], load_sem.at[g, way])

    def load_last(g):
        return pltpu.make_async_copy(chunk(g, 0, 0, REPS), last_own.at[g], load_sem.at[g, 2])

    def line_place(g, step):
        return ((y if g % 2 == 0 else x) + step) % SIDE

    def line(g, d):
        return send(line_sum.at[g, line_place(g, d)], line_in.at[g % 2, d - 1],
                    line_s.at[g % 2, d - 1], line_r.at[g % 2, d - 1], along(1 - g % 2, d))

    def lfar(g, way):
        return send(line_sum.at[g, line_place(g, 2), pl.ds(8 * way, 8)], line_far.at[g, way],
                    lfar_s.at[g, way], lfar_r.at[g, way], along(1 - g % 2, 1 - 2 * way))

    def lnear(g, way):
        return send(line_sum.at[g, line_place(g, 1 - 2 * way), pl.ds(8 - 8 * way, 8)],
                    line_near.at[g, way],
                    lnear_s.at[g, way], lnear_r.at[g, way], along(1 - g % 2, 1 - 2 * way))

    def lboth(g, way):
        return send(line_sum.at[g, line_place(g, 1 - 2 * way), pl.ds(8 * way, 8)],
                    line_both.at[g, way],
                    lboth_s.at[g, way], lboth_r.at[g, way], along(1 - g % 2, 1 - 2 * way))

    def direct(wide):
        return wide == STEPS - 1

    def start_far(wide):
        for g in (2 * wide, 2 * wide + 1):
            for way in range(2):
                far(g, way).start()
                load_near(g, way).start()

    def start_near(wide):
        for g in (2 * wide, 2 * wide + 1):
            for way in range(2):
                near(g, way).start()
            load_last(g).start()

    def combine(wide):
        for g in (2 * wide, 2 * wide + 1):
            for way in range(2):
                load_near(g, way).wait()
                far(g, way).wait_recv()

                @pl.loop(0, 8)
                def _(b):
                    near_own[g, way, b] = near_own[g, way, b] + far_in[g, way, b]

                both(g, way).start()

    def line_total(wide):
        for g in (2 * wide, 2 * wide + 1):
            load_last(g).wait()
            for way in range(2):
                near(g, way).wait_recv()
                both(g, way).wait_recv()

            @pl.loop(0, 8)
            def _(b):
                for way in range(2):
                    total = (last_own[g, 8 * way + b].astype(f32)
                             + both_in[g, way, b].astype(f32)
                             + near_in[g, 1 - way, b].astype(f32))
                    line_sum[g, :, 8 * way + b] = total.astype(bf16)

            if direct(wide):
                for d in (2, 1, 3):
                    line(g, d).start()
            else:
                for way in range(2):
                    lfar(g, way).start()
                for way in range(2):
                    lnear(g, way).start()

    def line_combine(wide):
        if direct(wide):
            return
        for g in (2 * wide, 2 * wide + 1):
            for way in range(2):
                lfar(g, way).wait_recv()
                place = line_place(g, 1 - 2 * way)

                @pl.loop(0, 8)
                def _(b):
                    line_sum[g, place, 8 * way + b] = (
                        line_sum[g, place, 8 * way + b] + line_far[g, way, b])

                lboth(g, way).start()

    def total(wide):
        for g in (2 * wide, 2 * wide + 1):
            place = line_place(g, 0)

            def finish(b, value):
                value = value.astype(bf16)
                piece[wide, b, pl.ds(g % 2 * HALF, HALF), :] = value
                value = value.astype(f32)
                value = value * value
                squares[...] += value[:8] + value[8:]

            if direct(wide):
                for d in (1, 2, 3):
                    line(g, d).wait_recv()

                @pl.loop(0, REPS)
                def _(b):
                    value = line_sum[g, place, b].astype(f32)
                    for d in range(3):
                        value = value + line_in[g % 2, d, b].astype(f32)
                    finish(b, value)
            else:
                for way in range(2):
                    lnear(g, way).wait_recv()
                    lboth(g, way).wait_recv()

                @pl.loop(0, 8)
                def _(b):
                    for way in range(2):
                        finish(8 * way + b,
                               line_sum[g, place, 8 * way + b].astype(f32)
                               + line_both[g, way, b].astype(f32)
                               + line_near[g, 1 - way, b].astype(f32))

    def columns(wide):
        return pl.ds(wide * WIDE, WIDE)

    def owner(wide, d):
        return send(to_owner.at[wide, (r + d) % REPS], block_in.at[:, r, :, columns(wide)],
                    owner_s.at[wide, d], owner_r.at[wide, d], other(d))

    def route(wide):
        @pl.loop(0, REPS)
        def _(o):
            for k in range(SLOTS):
                to_owner[wide, o, k] = piece[wide, table[0, o * SLOTS + k]]

        @pl.loop(1, REPS)
        def _(d):
            owner(wide, d).start()

        block_in[:, r, :, columns(wide)] = to_owner[wide, r]

    def wait_route(wide):
        @pl.loop(1, REPS)
        def _(d):
            owner(wide, d).wait_recv()

    roots = [pltpu.make_async_copy(ref, root_in.at[i], root_sem.at[i])
             for i, ref in enumerate((left_root, right_root))]
    stats = [pltpu.make_async_copy(ref, stat_in.at[i], stat_sem.at[i])
             for i, ref in enumerate((left_stat, right_stat))]

    names = pltpu.make_async_copy(owner_list, owners, list_sem)

    start_far(0)
    names.start()
    start_near(0)
    start_far(1)
    for copy in roots:
        copy.start()

    names.wait()

    @pl.loop(0, REPS)
    def _(j):
        mine = owners[0, s * REPS + j]
        count = jnp.int32(0)
        for i in range(REPS):
            hit = (owners[0, s * REPS + i] == mine) & (i < j)
            count = count + hit.astype(jnp.int32)
        table[1, j] = mine
        table[2, j] = jnp.minimum(count, SLOTS - 1)

    @pl.loop(0, REPS)
    def _(o):
        first, second = jnp.int32(REPS), jnp.int32(REPS)
        for j in range(REPS):
            hit = table[1, j] == o
            first = jnp.where(hit & (table[2, j] == 0), j, first)
            second = jnp.where(hit & (table[2, j] == 1), j, second)
        table[0, o * SLOTS] = first
        table[0, o * SLOTS + 1] = second

    for wide in range(STEPS):
        piece[wide, REPS] = jnp.zeros((PIECE, WIDE), bf16)
    squares[...] = jnp.zeros_like(squares)

    def split(side):
        roots[side].wait()

        @pl.loop(0, SLOTS * 8)
        def _(i):
            k, t = i // 8, i % 8
            rows = pl.ds(pl.multiple_of(t * 64, 64), 64)
            whole = root_in[side, k, rows, :]
            top = whole.astype(bf16)
            root_hi[side, k, rows, :] = top
            root_lo[side, k, rows, :] = (whole - top.astype(f32)).astype(bf16)

    for wide in range(STEPS):
        combine(wide)
        if wide + 1 < STEPS:
            start_near(wide + 1)
        if wide + 2 < STEPS:
            start_far(wide + 2)
        if wide < 2:
            split(wide)
        line_total(wide)
        if wide == 0:
            for copy in stats:
                copy.start()
        if wide >= 1:
            line_combine(wide - 1)
        if wide >= 2:
            total(wide - 2)
            route(wide - 2)
    line_combine(STEPS - 1)
    for wide in (STEPS - 2, STEPS - 1):
        total(wide)
        route(wide)

    def square(d):
        return send(squares, squares_in.at[d], square_s.at[d], square_r.at[d], other(d))

    @pl.loop(1, REPS)
    def _(d):
        square(d).start()

    def product(first, count):
        @pl.loop(0, SLOTS * 2)
        def _(i):
            t, k = i // 2, i % 2
            rows = pl.ds(pl.multiple_of(t * 256, 256), 256)
            across = pl.ds(first, count)
            block = block_in[k, :, :, across].reshape(BLOCK, count)
            part = (jnp.dot(root_hi[0, k, rows, :], block, preferred_element_type=f32)
                    + jnp.dot(root_lo[0, k, rows, :], block, preferred_element_type=f32))
            top = part.astype(bf16)
            low = (part - top.astype(f32)).astype(bf16)
            hi, lo = root_hi[1, k, across, :], root_lo[1, k, across, :]
            value = (jnp.dot(top, hi, preferred_element_type=f32)
                     + jnp.dot(top, lo, preferred_element_type=f32)
                     + jnp.dot(low, hi, preferred_element_type=f32))
            if first == 0:
                precond[k, rows, :] = value
            else:
                value = precond[k, rows, :] + value
                precond[k, rows, :] = value
            if first + count == BLOCK:
                ready[k, pl.ds(t * 8, 8)] = value.astype(bf16).reshape(8, PIECE, BLOCK)

    def gather_column(d, value):
        square(d).wait_recv()
        return value + squares_in[d]

    def column_send(to_root):
        if to_root is None:
            return send(column.at[0], column_in.at[s], column_s.at[0], column_r.at[s], (ROOT, r))
        place = (ROOT + to_root) % COLS
        return send(column.at[1], column_in.at[ROOT], column_s.at[to_root], column_r.at[ROOT], (place, r))

    def column_from(d):
        place = (ROOT + d) % COLS
        return send(column.at[0], column_in.at[place], column_s.at[0], column_r.at[place], (ROOT, r))

    wait_route(0)
    wait_route(1)
    product(0, 2 * WIDE)
    wait_route(2)
    product(2 * WIDE, WIDE)

    all_squares = lax.fori_loop(1, REPS, gather_column, squares[...])
    column[0] = jnp.sum(all_squares, axis=0, keepdims=True)

    @pl.when(s != ROOT)
    def _():
        column_send(None).start()

    wait_route(3)
    product(3 * WIDE, WIDE)

    def hold(turn, d):
        return send(ready.at[:, (r + d) % REPS, :, pl.ds(turn * BACK, BACK)], held[turn].at[r],
                    held_s.at[turn, d], held_r.at[turn, d], other(d))

    for turn in range(TURNS):
        @pl.loop(1, REPS)
        def _(d):
            hold(turn, d).start()

        held[turn][r] = ready[:, r, :, pl.ds(turn * BACK, BACK)]

    for k in range(SLOTS):
        def square_sum(i, carry):
            value, power = carry
            p = precond[k, pl.ds(pl.multiple_of(i * PIECE, PIECE), PIECE), :]
            g = block_in[k, i].astype(f32)
            return value + g * g, power + p * p

        zero = jnp.zeros((PIECE, BLOCK), f32)
        value, power = lax.fori_loop(0, REPS, square_sum, (zero, zero))
        value = jnp.sum(value, axis=(0, 1), keepdims=True) / (BLOCK * BLOCK)
        power = jnp.sum(power, axis=(0, 1), keepdims=True) / (BLOCK * BLOCK)
        scale = jnp.sqrt(value + epsilon) / jnp.sqrt(power + epsilon)
        scale_own[pl.ds(k, 1), :] = jnp.broadcast_to(scale, (1, 128))

    def scale_send(d):
        return send(scale_own, scale_in.at[r], scale_s.at[d], scale_r.at[d], other(d))

    @pl.loop(1, REPS)
    def _(d):
        scale_send(d).start()

    scale_in[r] = scale_own[...]

    @pl.when(s == ROOT)
    def _():
        def gather(d, value):
            column_from(d).wait_recv()
            return value + column_in[(ROOT + d) % COLS]

        column[1] = lax.fori_loop(1, COLS, gather, column[0])
        column_in[ROOT] = column[1]

        @pl.loop(1, COLS)
        def _(d):
            column_send(d).start()

    for copy in stats:
        copy.wait()

    @pl.loop(0, SLOTS)
    def _(k):
        filled = table[0, r * SLOTS + k] < REPS
        keep = jnp.where(filled, decay_keep, 1.0).astype(f32)
        weight = (1.0 - decay_keep) / BLOCK
        for t in range(2):
            rows = pl.ds(t * 256, 256)
            block = block_in[k].reshape(BLOCK, BLOCK)
            left = lax.dot_general(
                block[t * 256:(t + 1) * 256], block, (((1,), (1,)), ((), ())),
                preferred_element_type=f32)
            left_out[k, rows, :] = keep * stat_in[0, k, rows, :] + weight * left
            right = lax.dot_general(
                block[:, t * 256:(t + 1) * 256], block, (((0,), (0,)), ((), ())),
                preferred_element_type=f32)
            right_out[k, rows, :] = keep * stat_in[1, k, rows, :] + weight * right

    @pl.when(s != ROOT)
    def _():
        send(column.at[1], column_in.at[ROOT], column_s.at[1], column_r.at[ROOT], (ROOT, r)).wait_recv()

    rms = jnp.sqrt(jnp.sum(column_in[ROOT], axis=(0, 1), keepdims=True)
                   / (COLS * REPS * BLOCK * BLOCK))
    clip = jnp.minimum(1.0, rms_limit / rms)

    @pl.loop(1, REPS)
    def _(d):
        scale_send(d).wait_recv()

    def settle(turn, d):
        return send(to_place.at[turn, (r + d) % REPS], update.at[r, :, pl.ds(turn * BACK, BACK)],
                    place_s.at[turn, d], place_r.at[turn, d], other(d))

    for turn in range(TURNS):
        @pl.loop(1, REPS)
        def _(d):
            hold(turn, d).wait_recv()

        @pl.loop(0, REPS)
        def _(j):
            o, k = table[1, j], table[2, j]
            both_scales = scale_in[o]
            scale = jnp.where(k == 0, both_scales[:1], both_scales[1:]) * clip
            value = held[turn][o, k].astype(f32)
            for part in range(BACK // 128):
                to_place[turn, j, :, pl.ds(part * 128, 128)] = (
                    value[:, part * 128:(part + 1) * 128] * scale).astype(bf16)

        @pl.loop(1, REPS)
        def _(d):
            settle(turn, d).start()

        update[r, :, pl.ds(turn * BACK, BACK)] = to_place[turn, r]

    for g in range(2 * STEPS):
        for way in range(2):
            far(g, way).wait_send()
            near(g, way).wait_send()
            both(g, way).wait_send()
            if not direct(g // 2):
                lfar(g, way).wait_send()
                lnear(g, way).wait_send()
                lboth(g, way).wait_send()
        if direct(g // 2):
            for d in (1, 2, 3):
                line(g, d).wait_send()

    @pl.when(s != ROOT)
    def _():
        column_send(None).wait_send()

    @pl.when(s == ROOT)
    def _():
        @pl.loop(1, COLS)
        def _(d):
            column_send(d).wait_send()

    @pl.loop(1, REPS)
    def _(d):
        square(d).wait_send()
        scale_send(d).wait_send()
        for wide in range(STEPS):
            owner(wide, d).wait_send()
        for turn in range(TURNS):
            hold(turn, d).wait_send()
            settle(turn, d).wait_send()
            settle(turn, d).wait_recv()


def on_device(partial_grads, owner_list, left_stat, right_stat, left_root, right_root):
    grads = partial_grads.reshape(REPS, SIDE, SIDE, 2, HALF, BLOCK)
    hbm_spec = pl.BlockSpec(memory_space=pltpu.HBM)
    vmem_spec = pl.BlockSpec(memory_space=pltpu.VMEM)
    dma = pltpu.SemaphoreType.DMA
    groups = 2 * STEPS
    quarter = pltpu.VMEM((groups, 2, 8, SIDE, HALF, WIDE), bf16)
    eighth = pltpu.VMEM((groups, 2, 8, HALF, WIDE), bf16)
    pair = [dma((groups, 2))] * 2
    state = pltpu.VMEM((SLOTS, BLOCK, BLOCK), f32)
    update, left_new, right_new = pl.pallas_call(
        kernel,
        out_shape=(pltpu.VMEM((REPS, PIECE, BLOCK), bf16), state, state),
        in_specs=[hbm_spec] * 6,
        out_specs=(vmem_spec, vmem_spec, vmem_spec),
        scratch_shapes=[
            quarter, quarter, quarter, quarter,
            pltpu.VMEM((groups, REPS, SIDE, HALF, WIDE), bf16),
            pltpu.VMEM((groups, SIDE, REPS, HALF, WIDE), bf16),
            eighth, eighth, eighth,
            pltpu.VMEM((2, 3, REPS, HALF, WIDE), bf16),
            pltpu.VMEM((STEPS, REPS + 1, PIECE, WIDE), bf16),
            pltpu.VMEM((STEPS, REPS, SLOTS, PIECE, WIDE), bf16),
            pltpu.VMEM((SLOTS, REPS, PIECE, BLOCK), bf16),
            pltpu.VMEM((2, SLOTS, BLOCK, BLOCK), f32),
            pltpu.VMEM((2, SLOTS, BLOCK, BLOCK), bf16),
            pltpu.VMEM((2, SLOTS, BLOCK, BLOCK), bf16),
            pltpu.VMEM((2, SLOTS, BLOCK, BLOCK), f32),
            pltpu.VMEM((SLOTS, BLOCK, BLOCK), f32),
            pltpu.VMEM((SLOTS, REPS, PIECE, BLOCK), bf16),
            pltpu.VMEM((REPS, SLOTS, PIECE, BACK), bf16),
            pltpu.VMEM((REPS, SLOTS, PIECE, BACK), bf16),
            pltpu.VMEM((SLOTS, 128), f32),
            pltpu.VMEM((REPS, SLOTS, 128), f32),
            pltpu.VMEM((TURNS, REPS, PIECE, BACK), bf16),
            pltpu.VMEM((8, 128), f32),
            pltpu.VMEM((REPS, 8, 128), f32),
            pltpu.VMEM((2, 1, 128), f32),
            pltpu.VMEM((COLS, 1, 128), f32),
            pltpu.SMEM((1, COLS * REPS), jnp.int32),
            pltpu.SMEM((3, REPS * SLOTS), jnp.int32),
            dma((groups, 3)), dma((2,)), dma((2,)), dma,
        ] + pair * 6 + [dma((2, 3))] * 2 + [dma((STEPS, REPS))] * 2
        + [dma((TURNS, REPS))] * 2 + [dma((REPS,))] * 2 + [dma((TURNS, REPS))] * 2
        + [dma((REPS,))] * 2 + [dma((COLS,))] * 2,
        compiler_params=pltpu.CompilerParams(
            collective_id=0, has_side_effects=True, vmem_limit_bytes=58 << 20),
    )(grads, owner_list.reshape(1, COLS * REPS),
      left_stat[0, 0], right_stat[0, 0], left_root[0, 0], right_root[0, 0])
    return (update.reshape(1, BLOCK, BLOCK), left_new[None, None], right_new[None, None])


def solution(mesh):
    return jax.shard_map(
        on_device,
        mesh=mesh,
        in_specs=(
            P("replica", "shard", None, None),
            P(),
            P("shard", "replica", None, None, None),
            P("shard", "replica", None, None, None),
            P("shard", "replica", None, None, None),
            P("shard", "replica", None, None, None),
        ),
        out_specs=(
            P(("shard", "replica"), None, None),
            P("shard", "replica", None, None, None),
            P("shard", "replica", None, None, None),
        ),
        check_vma=False,
    )
```

```python
import functools

import jax
import jax.numpy as jnp
from jax import lax
from jax.experimental import pallas as pl
from jax.experimental.pallas import tpu as pltpu
from jax.sharding import PartitionSpec as P

decay_keep = 0.9
epsilon = 1e-06
rms_limit = 0.5

MESH = pl.DeviceIdType.MESH
f32 = jnp.float32
bf16 = jnp.bfloat16

SIDE = 4
REPS = 16
COLS = 8
ROOT = 1
SLOTS = 2
BLOCK = 512
PIECE = 32
HALF = 16
WIDE = 128
STEPS = BLOCK // WIDE
BACK = 256
TURNS = BLOCK // BACK


def kernel(
    grads, owner_list, left_stat, right_stat, left_root, right_root,
    update, left_out, right_out,
    far_in, pass_in, near_own, last_own,
    line_sum, line_far, line_pass, line_in, piece,
    to_owner, block_in, root_in, root_hi, root_lo, stat_in, precond, ready,
    held_first, held_last, scale_own, scale_in, to_place,
    squares, squares_in, column, column_in, owners, table,
    near_sem, last_sem, root_sem, stat_sem, list_sem,
    far_s, far_r, near_s, both_s, pass_r, lfar_s, lfar_r, lnear_s, lboth_s, lpass_r,
    line_s, line_r, owner_s, owner_r, held_s, held_r, scale_s, scale_r, place_s, place_r,
    square_s, square_r, column_s, column_r,
):
    s = lax.axis_index("shard")
    r = lax.axis_index("replica")
    x, y = r % SIDE, r // SIDE
    held = (held_first, held_last)

    def along(half, step):
        if half == 0:
            return (s, y * SIDE + (x + step) % SIDE)
        return (s, (y + step) % SIDE * SIDE + x)

    def other(d):
        return (s, (r + d) % REPS)

    def send(src, dst, send_sem, recv_sem, device):
        return pltpu.make_async_remote_copy(
            src_ref=src, dst_ref=dst, send_sem=send_sem, recv_sem=recv_sem,
            device_id=device, device_id_type=MESH,
        )

    def landed(ref, sem):
        send(ref, ref, column_s, sem, other(1)).wait_recv()

    def left(ref, sem):
        send(ref, ref, sem, column_r, other(1)).wait_send()

    def loaded(ref, sem):
        pltpu.make_async_copy(ref, ref, sem).wait()

    barrier = pltpu.get_barrier_semaphore()
    for half in range(2):
        for step in (1, 3):
            pl.semaphore_signal(barrier, inc=1, device_id=along(half, step), device_id_type=MESH)

    @pl.when(s == ROOT)
    def _():
        @pl.loop(1, COLS)
        def _(d):
            pl.semaphore_signal(barrier, inc=1, device_id=((s + d) % COLS, r), device_id_type=MESH)

        pl.semaphore_wait(barrier, 4)

    @pl.when(s != ROOT)
    def _():
        pl.semaphore_wait(barrier, 5)

    def chunk(g, step, first, count):
        wide, half = g // 2, g % 2
        place = ((x if half == 0 else y) + step) % SIDE
        rows = pl.ds(first, count)
        cols = pl.ds(wide * WIDE, WIDE)
        if half == 0:
            return grads.at[rows, :, place, 0, :, cols]
        return grads.at[rows, place, :, 1, :, cols]

    def far(g, way):
        return send(chunk(g, 2, 8 * way, 8), far_in.at[g, way],
                    far_s, far_r.at[g // 2], along(g % 2, 1 - 2 * way))

    def near(g, way):
        return send(chunk(g, 1 - 2 * way, 8 - 8 * way, 8), pass_in.at[g, 0, way],
                    near_s, pass_r.at[g // 2], along(g % 2, 1 - 2 * way))

    def both(g, way):
        return send(near_own.at[g, way], pass_in.at[g, 1, way],
                    both_s, pass_r.at[g // 2], along(g % 2, 1 - 2 * way))

    def load_near(g, way):
        return pltpu.make_async_copy(chunk(g, 1 - 2 * way, 8 * way, 8),
                                     near_own.at[g, way], near_sem.at[g // 2])

    def load_last(g):
        return pltpu.make_async_copy(chunk(g, 0, 0, REPS), last_own.at[g], last_sem.at[g // 2])

    def line_place(g, step):
        return ((y if g % 2 == 0 else x) + step) % SIDE

    def line(g, d):
        return send(line_sum.at[g, line_place(g, d)], line_in.at[g % 2, d - 1],
                    line_s, line_r, along(1 - g % 2, d))

    def lfar(g, way):
        return send(line_sum.at[g, line_place(g, 2), pl.ds(8 * way, 8)], line_far.at[g, way],
                    lfar_s, lfar_r.at[g // 2], along(1 - g % 2, 1 - 2 * way))

    def lnear(g, way):
        return send(line_sum.at[g, line_place(g, 1 - 2 * way), pl.ds(8 - 8 * way, 8)],
                    line_pass.at[g, 0, way],
                    lnear_s, lpass_r.at[g // 2], along(1 - g % 2, 1 - 2 * way))

    def lboth(g, way):
        return send(line_sum.at[g, line_place(g, 1 - 2 * way), pl.ds(8 * way, 8)],
                    line_pass.at[g, 1, way],
                    lboth_s, lpass_r.at[g // 2], along(1 - g % 2, 1 - 2 * way))

    def pair(wide):
        return pl.ds(2 * wide, 2)

    def direct(wide):
        return wide == STEPS - 1

    def start_far(wide):
        for g in (2 * wide, 2 * wide + 1):
            for way in range(2):
                far(g, way).start()
                load_near(g, way).start()

    def start_near(wide):
        for g in (2 * wide, 2 * wide + 1):
            for way in range(2):
                near(g, way).start()
            load_last(g).start()

    def combine(wide):
        loaded(near_own.at[pair(wide)], near_sem.at[wide])
        landed(far_in.at[pair(wide)], far_r.at[wide])
        for g in (2 * wide, 2 * wide + 1):
            for way in range(2):
                @pl.loop(0, 8)
                def _(b):
                    near_own[g, way, b] = near_own[g, way, b] + far_in[g, way, b]

                both(g, way).start()

    def line_total(wide):
        loaded(last_own.at[pair(wide)], last_sem.at[wide])
        landed(pass_in.at[pair(wide)], pass_r.at[wide])
        for g in (2 * wide, 2 * wide + 1):
            @pl.loop(0, 8)
            def _(b):
                for way in range(2):
                    total = (last_own[g, 8 * way + b].astype(f32)
                             + pass_in[g, 1, way, b].astype(f32)
                             + pass_in[g, 0, 1 - way, b].astype(f32))
                    line_sum[g, :, 8 * way + b] = total.astype(bf16)

            if direct(wide):
                for d in (2, 1, 3):
                    line(g, d).start()
            else:
                for way in range(2):
                    lfar(g, way).start()
                for way in range(2):
                    lnear(g, way).start()

    def line_combine(wide):
        landed(line_far.at[pair(wide)], lfar_r.at[wide])
        for g in (2 * wide, 2 * wide + 1):
            for way in range(2):
                place = line_place(g, 1 - 2 * way)

                @pl.loop(0, 8)
                def _(b):
                    line_sum[g, place, 8 * way + b] = (
                        line_sum[g, place, 8 * way + b] + line_far[g, way, b])

                lboth(g, way).start()

    def total(wide):
        if direct(wide):
            landed(line_in, line_r)
        else:
            landed(line_pass.at[pair(wide)], lpass_r.at[wide])
        for g in (2 * wide, 2 * wide + 1):
            place = line_place(g, 0)

            def finish(b, value):
                value = value.astype(bf16)
                piece[wide, b, pl.ds(g % 2 * HALF, HALF), :] = value
                value = value.astype(f32)
                value = value * value
                squares[...] += value[:8] + value[8:]

            if direct(wide):
                @pl.loop(0, REPS)
                def _(b):
                    value = line_sum[g, place, b].astype(f32)
                    for d in range(3):
                        value = value + line_in[g % 2, d, b].astype(f32)
                    finish(b, value)
            else:
                @pl.loop(0, 8)
                def _(b):
                    for way in range(2):
                        finish(8 * way + b,
                               line_sum[g, place, 8 * way + b].astype(f32)
                               + line_pass[g, 1, way, b].astype(f32)
                               + line_pass[g, 0, 1 - way, b].astype(f32))

    def columns(wide):
        return pl.ds(wide * WIDE, WIDE)

    def owner(wide, d):
        return send(to_owner.at[wide, (r + d) % REPS], block_in.at[:, r, :, columns(wide)],
                    owner_s, owner_r.at[wide], other(d))

    def route(wide):
        @pl.loop(0, REPS)
        def _(o):
            for k in range(SLOTS):
                to_owner[wide, o, k] = piece[wide, table[0, o * SLOTS + k]]

        @pl.loop(1, REPS)
        def _(d):
            owner(wide, d).start()

        block_in[:, r, :, columns(wide)] = to_owner[wide, r]

    def wait_route(wide):
        landed(block_in.at[:, pl.ds(0, REPS - 1), :, columns(wide)], owner_r.at[wide])

    roots = [pltpu.make_async_copy(ref, root_in.at[i], root_sem.at[i])
             for i, ref in enumerate((left_root, right_root))]
    stats = [pltpu.make_async_copy(ref, stat_in.at[i], stat_sem.at[i])
             for i, ref in enumerate((left_stat, right_stat))]

    names = pltpu.make_async_copy(owner_list, owners, list_sem)

    start_far(0)
    names.start()
    start_near(0)
    start_far(1)
    for copy in roots:
        copy.start()

    names.wait()

    @pl.loop(0, REPS)
    def _(j):
        mine = owners[0, s * REPS + j]
        count = jnp.int32(0)
        for i in range(REPS):
            hit = (owners[0, s * REPS + i] == mine) & (i < j)
            count = count + hit.astype(jnp.int32)
        table[1, j] = mine
        table[2, j] = jnp.minimum(count, SLOTS - 1)

    @pl.loop(0, REPS)
    def _(o):
        first, second = jnp.int32(REPS), jnp.int32(REPS)
        for j in range(REPS):
            hit = table[1, j] == o
            first = jnp.where(hit & (table[2, j] == 0), j, first)
            second = jnp.where(hit & (table[2, j] == 1), j, second)
        table[0, o * SLOTS] = first
        table[0, o * SLOTS + 1] = second

    for wide in range(STEPS):
        piece[wide, REPS] = jnp.zeros((PIECE, WIDE), bf16)
    squares[...] = jnp.zeros_like(squares)

    def split(side):
        roots[side].wait()

        @pl.loop(0, SLOTS * 8)
        def _(i):
            k, t = i // 8, i % 8
            rows = pl.ds(pl.multiple_of(t * 64, 64), 64)
            whole = root_in[side, k, rows, :]
            top = whole.astype(bf16)
            root_hi[side, k, rows, :] = top
            root_lo[side, k, rows, :] = (whole - top.astype(f32)).astype(bf16)

    for wide in range(STEPS):
        combine(wide)
        if wide + 1 < STEPS:
            start_near(wide + 1)
        if wide + 2 < STEPS:
            start_far(wide + 2)
        if wide < 2:
            split(wide)
        if wide >= 1:
            line_combine(wide - 1)
        line_total(wide)
        if wide == 0:
            for copy in stats:
                copy.start()
        if wide >= 1:
            total(wide - 1)
            route(wide - 1)
    total(STEPS - 1)
    route(STEPS - 1)

    def square(d):
        return send(squares, squares_in.at[d], square_s, square_r, other(d))

    @pl.loop(1, REPS)
    def _(d):
        square(d).start()

    def product(first, count):
        @pl.loop(0, SLOTS * 2)
        def _(i):
            t, k = i // 2, i % 2
            rows = pl.ds(pl.multiple_of(t * 256, 256), 256)
            across = pl.ds(first, count)
            block = block_in[k, :, :, across].reshape(BLOCK, count)
            part = (jnp.dot(root_hi[0, k, rows, :], block, preferred_element_type=f32)
                    + jnp.dot(root_lo[0, k, rows, :], block, preferred_element_type=f32))
            top = part.astype(bf16)
            low = (part - top.astype(f32)).astype(bf16)
            hi, lo = root_hi[1, k, across, :], root_lo[1, k, across, :]
            value = (jnp.dot(top, hi, preferred_element_type=f32)
                     + jnp.dot(top, lo, preferred_element_type=f32)
                     + jnp.dot(low, hi, preferred_element_type=f32))
            if first == 0:
                precond[k, rows, :] = value
            else:
                value = precond[k, rows, :] + value
                precond[k, rows, :] = value
            if first + count == BLOCK:
                ready[k, pl.ds(t * 8, 8)] = value.astype(bf16).reshape(8, PIECE, BLOCK)

    def gather_column(d, value):
        return value + squares_in[d]

    def column_in_root():
        return send(column.at[0], column_in.at[s], column_s, column_r, (ROOT, r))

    def column_out(d):
        return send(column.at[1], column_in.at[ROOT], column_s, column_r, ((ROOT + d) % COLS, r))

    wait_route(0)
    wait_route(1)
    product(0, 2 * WIDE)
    wait_route(2)
    product(2 * WIDE, WIDE)

    landed(squares_in.at[pl.ds(1, REPS - 1)], square_r)
    all_squares = lax.fori_loop(1, REPS, gather_column, squares[...])
    column[0] = jnp.sum(all_squares, axis=0, keepdims=True)

    @pl.when(s != ROOT)
    def _():
        column_in_root().start()

    wait_route(3)
    product(3 * WIDE, WIDE)

    def hold(turn, d):
        return send(ready.at[:, (r + d) % REPS, :, pl.ds(turn * BACK, BACK)], held[turn].at[r],
                    held_s, held_r.at[turn], other(d))

    for turn in range(TURNS):
        @pl.loop(1, REPS)
        def _(d):
            hold(turn, d).start()

        held[turn][r] = ready[:, r, :, pl.ds(turn * BACK, BACK)]

    for k in range(SLOTS):
        def square_sum(i, carry):
            value, power = carry
            p = precond[k, pl.ds(pl.multiple_of(i * PIECE, PIECE), PIECE), :]
            g = block_in[k, i].astype(f32)
            return value + g * g, power + p * p

        zero = jnp.zeros((PIECE, BLOCK), f32)
        value, power = lax.fori_loop(0, REPS, square_sum, (zero, zero))
        value = jnp.sum(value, axis=(0, 1), keepdims=True) / (BLOCK * BLOCK)
        power = jnp.sum(power, axis=(0, 1), keepdims=True) / (BLOCK * BLOCK)
        scale = jnp.sqrt(value + epsilon) / jnp.sqrt(power + epsilon)
        scale_own[pl.ds(k, 1), :] = jnp.broadcast_to(scale, (1, 128))

    def scale_send(d):
        return send(scale_own, scale_in.at[r], scale_s, scale_r, other(d))

    @pl.loop(1, REPS)
    def _(d):
        scale_send(d).start()

    scale_in[r] = scale_own[...]

    @pl.when(s == ROOT)
    def _():
        landed(column_in.at[pl.ds(0, COLS - 1)], column_r)

        def gather(d, value):
            return value + column_in[(ROOT + d) % COLS]

        column[1] = lax.fori_loop(1, COLS, gather, column[0])
        column_in[ROOT] = column[1]

        @pl.loop(1, COLS)
        def _(d):
            column_out(d).start()

    for copy in stats:
        copy.wait()

    @pl.loop(0, SLOTS)
    def _(k):
        filled = table[0, r * SLOTS + k] < REPS
        keep = jnp.where(filled, decay_keep, 1.0).astype(f32)
        weight = (1.0 - decay_keep) / BLOCK
        for t in range(2):
            rows = pl.ds(t * 256, 256)
            block = block_in[k].reshape(BLOCK, BLOCK)
            left = lax.dot_general(
                block[t * 256:(t + 1) * 256], block, (((1,), (1,)), ((), ())),
                preferred_element_type=f32)
            left_out[k, rows, :] = keep * stat_in[0, k, rows, :] + weight * left
            right = lax.dot_general(
                block[:, t * 256:(t + 1) * 256], block, (((0,), (0,)), ((), ())),
                preferred_element_type=f32)
            right_out[k, rows, :] = keep * stat_in[1, k, rows, :] + weight * right

    @pl.when(s != ROOT)
    def _():
        landed(column_in.at[ROOT], column_r)

    rms = jnp.sqrt(jnp.sum(column_in[ROOT], axis=(0, 1), keepdims=True)
                   / (COLS * REPS * BLOCK * BLOCK))
    clip = jnp.minimum(1.0, rms_limit / rms)

    landed(scale_in.at[pl.ds(0, REPS - 1)], scale_r)

    def settle(turn, d):
        return send(to_place.at[turn, (r + d) % REPS], update.at[r, :, pl.ds(turn * BACK, BACK)],
                    place_s, place_r, other(d))

    for turn in range(TURNS):
        landed(held[turn].at[pl.ds(0, REPS - 1)], held_r.at[turn])

        @pl.loop(0, REPS)
        def _(j):
            o, k = table[1, j], table[2, j]
            both_scales = scale_in[o]
            scale = jnp.where(k == 0, both_scales[:1], both_scales[1:]) * clip
            value = held[turn][o, k].astype(f32)
            for part in range(BACK // 128):
                to_place[turn, j, :, pl.ds(part * 128, 128)] = (
                    value[:, part * 128:(part + 1) * 128] * scale).astype(bf16)

        @pl.loop(1, REPS)
        def _(d):
            settle(turn, d).start()

        update[r, :, pl.ds(turn * BACK, BACK)] = to_place[turn, r]

    left(far_in, far_s)
    left(near_own, near_s)
    left(near_own, both_s)
    left(line_far, lfar_s)
    left(line_far, lnear_s)
    left(line_far, lboth_s)
    left(line_in, line_s)
    left(to_owner.at[:, pl.ds(0, REPS - 1)], owner_s)
    left(ready.at[:, pl.ds(0, REPS - 1)], held_s)
    left(to_place.at[:, pl.ds(0, REPS - 1)], place_s)
    left(squares_in.at[pl.ds(1, REPS - 1)], square_s)
    left(scale_in.at[pl.ds(0, REPS - 1)], scale_s)

    @pl.when(s != ROOT)
    def _():
        left(column_in.at[ROOT], column_s)

    @pl.when(s == ROOT)
    def _():
        left(column_in.at[pl.ds(0, COLS - 1)], column_s)

    landed(update.at[pl.ds(0, REPS - 1)], place_r)


def on_device(partial_grads, owner_list, left_stat, right_stat, left_root, right_root):
    grads = partial_grads.reshape(REPS, SIDE, SIDE, 2, HALF, BLOCK)
    hbm_spec = pl.BlockSpec(memory_space=pltpu.HBM)
    vmem_spec = pl.BlockSpec(memory_space=pltpu.VMEM)
    dma = pltpu.SemaphoreType.DMA
    groups = 2 * STEPS
    lines = groups - 2
    quarter = (2, 8, SIDE, HALF, WIDE)
    eighth = (2, 8, HALF, WIDE)
    state = pltpu.VMEM((SLOTS, BLOCK, BLOCK), f32)
    update, left_new, right_new = pl.pallas_call(
        kernel,
        out_shape=(pltpu.VMEM((REPS, PIECE, BLOCK), bf16), state, state),
        in_specs=[hbm_spec] * 6,
        out_specs=(vmem_spec, vmem_spec, vmem_spec),
        scratch_shapes=[
            pltpu.VMEM((groups,) + quarter, bf16),
            pltpu.VMEM((groups, 2) + quarter, bf16),
            pltpu.VMEM((groups,) + quarter, bf16),
            pltpu.VMEM((groups, REPS, SIDE, HALF, WIDE), bf16),
            pltpu.VMEM((groups, SIDE, REPS, HALF, WIDE), bf16),
            pltpu.VMEM((lines,) + eighth, bf16),
            pltpu.VMEM((lines, 2) + eighth, bf16),
            pltpu.VMEM((2, 3, REPS, HALF, WIDE), bf16),
            pltpu.VMEM((STEPS, REPS + 1, PIECE, WIDE), bf16),
            pltpu.VMEM((STEPS, REPS, SLOTS, PIECE, WIDE), bf16),
            pltpu.VMEM((SLOTS, REPS, PIECE, BLOCK), bf16),
            pltpu.VMEM((2, SLOTS, BLOCK, BLOCK), f32),
            pltpu.VMEM((2, SLOTS, BLOCK, BLOCK), bf16),
            pltpu.VMEM((2, SLOTS, BLOCK, BLOCK), bf16),
            pltpu.VMEM((2, SLOTS, BLOCK, BLOCK), f32),
            pltpu.VMEM((SLOTS, BLOCK, BLOCK), f32),
            pltpu.VMEM((SLOTS, REPS, PIECE, BLOCK), bf16),
            pltpu.VMEM((REPS, SLOTS, PIECE, BACK), bf16),
            pltpu.VMEM((REPS, SLOTS, PIECE, BACK), bf16),
            pltpu.VMEM((SLOTS, 128), f32),
            pltpu.VMEM((REPS, SLOTS, 128), f32),
            pltpu.VMEM((TURNS, REPS, PIECE, BACK), bf16),
            pltpu.VMEM((8, 128), f32),
            pltpu.VMEM((REPS, 8, 128), f32),
            pltpu.VMEM((2, 1, 128), f32),
            pltpu.VMEM((COLS, 1, 128), f32),
            pltpu.SMEM((1, COLS * REPS), jnp.int32),
            pltpu.SMEM((3, REPS * SLOTS), jnp.int32),
            dma((STEPS,)), dma((STEPS,)), dma((2,)), dma((2,)), dma,
            dma, dma((STEPS,)), dma, dma, dma((STEPS,)),
            dma, dma((STEPS - 1,)), dma, dma, dma((STEPS - 1,)),
            dma, dma, dma, dma((STEPS,)),
            dma, dma((TURNS,)), dma, dma, dma, dma,
            dma, dma, dma, dma,
        ],
        compiler_params=pltpu.CompilerParams(
            collective_id=0, has_side_effects=True, vmem_limit_bytes=58 << 20),
    )(grads, owner_list.reshape(1, COLS * REPS),
      left_stat[0, 0], right_stat[0, 0], left_root[0, 0], right_root[0, 0])
    return (update.reshape(1, BLOCK, BLOCK), left_new[None, None], right_new[None, None])


def solution(mesh):
    return jax.shard_map(
        on_device,
        mesh=mesh,
        in_specs=(
            P("replica", "shard", None, None),
            P(),
            P("shard", "replica", None, None, None),
            P("shard", "replica", None, None, None),
            P("shard", "replica", None, None, None),
            P("shard", "replica", None, None, None),
        ),
        out_specs=(
            P(("shard", "replica"), None, None),
            P("shard", "replica", None, None, None),
            P("shard", "replica", None, None, None),
        ),
        check_vma=False,
    )
```

```python
import functools

import jax
import jax.numpy as jnp
from jax import lax
from jax.experimental import pallas as pl
from jax.experimental.pallas import tpu as pltpu
from jax.sharding import PartitionSpec as P

decay_keep = 0.9
epsilon = 1e-06
rms_limit = 0.5

MESH = pl.DeviceIdType.MESH
f32 = jnp.float32
bf16 = jnp.bfloat16

SIDE = 4
REPS = 16
COLS = 8
ROOT = 1
SLOTS = 2
BLOCK = 512
PIECE = 32
HALF = 16
WIDE = 128
STEPS = BLOCK // WIDE
BACK = 256
TURNS = BLOCK // BACK


def kernel(
    grads, owner_list, left_stat, right_stat, left_root, right_root,
    update, left_out, right_out,
    far_in, pass_in, near_own, last_own,
    line_sum, line_far, line_pass, line_in, piece,
    to_first, to_second, block_in, root_in, root_hi, root_lo, stat_in, precond, ready,
    held_first, held_0, held_1, scale_own, scale_in, to_place,
    squares, squares_in, column, column_in, owners, table,
    near_sem, last_sem, root_sem, stat_sem, list_sem,
    far_s, far_r, near_s, both_s, pass_r, lfar_s, lfar_r, lnear_s, lboth_s, lpass_r,
    line_s, line_r, owner_s, owner_r, held_s, held_r, scale_s, scale_r, place_s, place_r,
    square_s, square_r, column_s, column_r,
):
    s = lax.axis_index("shard")
    r = lax.axis_index("replica")
    x, y = r % SIDE, r // SIDE
    held = (held_0, held_1)

    def along(half, step):
        if half == 0:
            return (s, y * SIDE + (x + step) % SIDE)
        return (s, (y + step) % SIDE * SIDE + x)

    def peer(d):
        return (r + d) % REPS

    def other(d):
        return (s, peer(d))

    def send(src, dst, send_sem, recv_sem, device):
        return pltpu.make_async_remote_copy(
            src_ref=src, dst_ref=dst, send_sem=send_sem, recv_sem=recv_sem,
            device_id=device, device_id_type=MESH,
        )

    def landed(ref, sem):
        send(ref, ref, column_s, sem, other(1)).wait_recv()

    def left(ref, sem):
        send(ref, ref, sem, column_r, other(1)).wait_send()

    def loaded(ref, sem):
        pltpu.make_async_copy(ref, ref, sem).wait()

    barrier = pltpu.get_barrier_semaphore()
    for half in range(2):
        for step in (1, 3):
            pl.semaphore_signal(barrier, inc=1, device_id=along(half, step), device_id_type=MESH)

    @pl.when(s == ROOT)
    def _():
        @pl.loop(1, COLS)
        def _(d):
            pl.semaphore_signal(barrier, inc=1, device_id=((s + d) % COLS, r), device_id_type=MESH)

        pl.semaphore_wait(barrier, 4)

    @pl.when(s != ROOT)
    def _():
        pl.semaphore_wait(barrier, 5)

    def chunk(g, step, first, count):
        wide, half = g // 2, g % 2
        place = ((x if half == 0 else y) + step) % SIDE
        rows = pl.ds(first, count)
        cols = pl.ds(wide * WIDE, WIDE)
        if half == 0:
            return grads.at[rows, :, place, 0, :, cols]
        return grads.at[rows, place, :, 1, :, cols]

    def far(g, way):
        return send(chunk(g, 2, 8 * way, 8), far_in.at[g, way],
                    far_s, far_r.at[g // 2], along(g % 2, 1 - 2 * way))

    def near(g, way):
        return send(chunk(g, 1 - 2 * way, 8 - 8 * way, 8), pass_in.at[g, 0, way],
                    near_s, pass_r.at[g // 2], along(g % 2, 1 - 2 * way))

    def both(g, way):
        return send(near_own.at[g, way], pass_in.at[g, 1, way],
                    both_s, pass_r.at[g // 2], along(g % 2, 1 - 2 * way))

    def load_near(g, way):
        return pltpu.make_async_copy(chunk(g, 1 - 2 * way, 8 * way, 8),
                                     near_own.at[g, way], near_sem.at[g // 2])

    def load_last(g):
        return pltpu.make_async_copy(chunk(g, 0, 0, REPS), last_own.at[g], last_sem.at[g // 2])

    def line_place(g, step):
        return ((y if g % 2 == 0 else x) + step) % SIDE

    def line(g, d):
        return send(line_sum.at[g, line_place(g, d)], line_in.at[g % 2, d - 1],
                    line_s, line_r, along(1 - g % 2, d))

    def lfar(g, way):
        return send(line_sum.at[g, line_place(g, 2), pl.ds(8 * way, 8)], line_far.at[g, way],
                    lfar_s, lfar_r.at[g // 2], along(1 - g % 2, 1 - 2 * way))

    def lnear(g, way):
        return send(line_sum.at[g, line_place(g, 1 - 2 * way), pl.ds(8 - 8 * way, 8)],
                    line_pass.at[g, 0, way],
                    lnear_s, lpass_r.at[g // 2], along(1 - g % 2, 1 - 2 * way))

    def lboth(g, way):
        return send(line_sum.at[g, line_place(g, 1 - 2 * way), pl.ds(8 * way, 8)],
                    line_pass.at[g, 1, way],
                    lboth_s, lpass_r.at[g // 2], along(1 - g % 2, 1 - 2 * way))

    def pair(wide):
        return pl.ds(2 * wide, 2)

    def direct(wide):
        return wide == STEPS - 1

    def start_far(wide):
        for g in (2 * wide, 2 * wide + 1):
            for way in range(2):
                far(g, way).start()
                load_near(g, way).start()

    def start_near(wide):
        for g in (2 * wide, 2 * wide + 1):
            for way in range(2):
                near(g, way).start()
            load_last(g).start()

    def combine(wide):
        loaded(near_own.at[pair(wide)], near_sem.at[wide])
        landed(far_in.at[pair(wide)], far_r.at[wide])
        for g in (2 * wide, 2 * wide + 1):
            for way in range(2):
                @pl.loop(0, 8)
                def _(b):
                    near_own[g, way, b] = near_own[g, way, b] + far_in[g, way, b]

                both(g, way).start()

    def line_total(wide):
        loaded(last_own.at[pair(wide)], last_sem.at[wide])
        landed(pass_in.at[pair(wide)], pass_r.at[wide])
        for g in (2 * wide, 2 * wide + 1):
            @pl.loop(0, 8)
            def _(b):
                for way in range(2):
                    total = (last_own[g, 8 * way + b].astype(f32)
                             + pass_in[g, 1, way, b].astype(f32)
                             + pass_in[g, 0, 1 - way, b].astype(f32))
                    line_sum[g, :, 8 * way + b] = total.astype(bf16)

            if direct(wide):
                for d in (2, 1, 3):
                    line(g, d).start()
            else:
                for way in range(2):
                    lfar(g, way).start()
                for way in range(2):
                    lnear(g, way).start()

    def line_combine(wide):
        landed(line_far.at[pair(wide)], lfar_r.at[wide])
        for g in (2 * wide, 2 * wide + 1):
            for way in range(2):
                place = line_place(g, 1 - 2 * way)

                @pl.loop(0, 8)
                def _(b):
                    line_sum[g, place, 8 * way + b] = (
                        line_sum[g, place, 8 * way + b] + line_far[g, way, b])

                lboth(g, way).start()

    def total(wide):
        if direct(wide):
            landed(line_in, line_r)
        else:
            landed(line_pass.at[pair(wide)], lpass_r.at[wide])
        for g in (2 * wide, 2 * wide + 1):
            place = line_place(g, 0)

            def finish(b, value):
                value = value.astype(bf16)
                piece[wide, b, pl.ds(g % 2 * HALF, HALF), :] = value
                value = value.astype(f32)
                value = value * value
                squares[...] += value[:8] + value[8:]

            if direct(wide):
                @pl.loop(0, REPS)
                def _(b):
                    value = line_sum[g, place, b].astype(f32)
                    for d in range(3):
                        value = value + line_in[g % 2, d, b].astype(f32)
                    finish(b, value)
            else:
                @pl.loop(0, 8)
                def _(b):
                    for way in range(2):
                        finish(8 * way + b,
                               line_sum[g, place, 8 * way + b].astype(f32)
                               + line_pass[g, 1, way, b].astype(f32)
                               + line_pass[g, 0, 1 - way, b].astype(f32))

    def columns(wide):
        return pl.ds(wide * WIDE, WIDE)

    def owner_first(wide, d):
        return send(to_first.at[wide, peer(d)], block_in.at[0, r, :, columns(wide)],
                    owner_s.at[0], owner_r.at[wide], other(d))

    def owner_second(turn, d):
        return send(to_second.at[turn, peer(d)], block_in.at[1, r, :, pl.ds(turn * BACK, BACK)],
                    owner_s.at[1], owner_r.at[STEPS + turn], other(d))

    def route_first(wide):
        @pl.loop(0, REPS)
        def _(o):
            to_first[wide, o] = piece[wide, table[0, o * SLOTS]]

        @pl.loop(1, REPS)
        def _(d):
            owner_first(wide, d).start()

        block_in[0, r, :, columns(wide)] = to_first[wide, r]

    def route_second(turn):
        each = BACK // WIDE

        @pl.loop(0, REPS)
        def _(o):
            for i in range(each):
                to_second[turn, o, :, pl.ds(i * WIDE, WIDE)] = (
                    piece[turn * each + i, table[0, o * SLOTS + 1]])

        @pl.loop(1, REPS)
        def _(d):
            owner_second(turn, d).start()

        block_in[1, r, :, pl.ds(turn * BACK, BACK)] = to_second[turn, r]

    def wait_first(wide):
        landed(block_in.at[0, pl.ds(0, REPS - 1), :, columns(wide)], owner_r.at[wide])

    def wait_second(turn):
        landed(block_in.at[1, pl.ds(0, REPS - 1), :, pl.ds(turn * BACK, BACK)],
               owner_r.at[STEPS + turn])

    roots = [pltpu.make_async_copy(ref, root_in.at[i], root_sem.at[i])
             for i, ref in enumerate((left_root, right_root))]
    stats = [pltpu.make_async_copy(ref, stat_in.at[i], stat_sem.at[i])
             for i, ref in enumerate((left_stat, right_stat))]

    names = pltpu.make_async_copy(owner_list, owners, list_sem)

    start_far(0)
    names.start()
    start_near(0)
    start_far(1)
    for copy in roots:
        copy.start()

    names.wait()

    @pl.loop(0, REPS)
    def _(j):
        mine = owners[0, s * REPS + j]
        count = jnp.int32(0)
        for i in range(REPS):
            hit = (owners[0, s * REPS + i] == mine) & (i < j)
            count = count + hit.astype(jnp.int32)
        table[1, j] = mine
        table[2, j] = jnp.minimum(count, SLOTS - 1)

    @pl.loop(0, REPS)
    def _(o):
        first, second = jnp.int32(REPS), jnp.int32(REPS)
        for j in range(REPS):
            hit = table[1, j] == o
            first = jnp.where(hit & (table[2, j] == 0), j, first)
            second = jnp.where(hit & (table[2, j] == 1), j, second)
        table[0, o * SLOTS] = first
        table[0, o * SLOTS + 1] = second

    for wide in range(STEPS):
        piece[wide, REPS] = jnp.zeros((PIECE, WIDE), bf16)
    squares[...] = jnp.zeros_like(squares)

    def split(side):
        roots[side].wait()

        @pl.loop(0, SLOTS * 8)
        def _(i):
            k, t = i // 8, i % 8
            rows = pl.ds(pl.multiple_of(t * 64, 64), 64)
            whole = root_in[side, k, rows, :]
            top = whole.astype(bf16)
            root_hi[side, k, rows, :] = top
            root_lo[side, k, rows, :] = (whole - top.astype(f32)).astype(bf16)

    combine(0)
    start_near(1)
    start_far(2)
    for side in range(2):
        split(side)
    for wide in range(STEPS):
        if wide + 1 < STEPS:
            combine(wide + 1)
        if wide + 2 < STEPS:
            start_near(wide + 2)
        if wide + 3 < STEPS:
            start_far(wide + 3)
        if wide >= 1:
            line_combine(wide - 1)
        line_total(wide)
        if wide == 0:
            for copy in stats:
                copy.start()
        if wide >= 1:
            total(wide - 1)
        if wide >= 2:
            route_first(wide - 2)
    route_first(STEPS - 2)
    route_second(0)
    total(STEPS - 1)
    route_first(STEPS - 1)

    def square(d):
        return send(squares_in.at[0], squares_in.at[d], square_s, square_r, other(d))

    squares_in[0] = jnp.sum(squares[...], axis=0, keepdims=True)

    @pl.loop(1, REPS)
    def _(d):
        square(d).start()

    route_second(1)


    def product(k, first, count):
        @pl.loop(0, 2)
        def _(t):
            rows = pl.ds(pl.multiple_of(t * 256, 256), 256)
            across = pl.ds(first, count)
            block = block_in[k, :, :, across].reshape(BLOCK, count)
            part = (jnp.dot(root_hi[0, k, rows, :], block, preferred_element_type=f32)
                    + jnp.dot(root_lo[0, k, rows, :], block, preferred_element_type=f32))
            top = part.astype(bf16)
            low = (part - top.astype(f32)).astype(bf16)
            hi, lo = root_hi[1, k, across, :], root_lo[1, k, across, :]
            value = (jnp.dot(top, hi, preferred_element_type=f32)
                     + jnp.dot(top, lo, preferred_element_type=f32)
                     + jnp.dot(low, hi, preferred_element_type=f32))
            if first > 0:
                value = precond[k, rows, :] + value
            precond[k, rows, :] = value
            if first + count == BLOCK:
                ready[k, pl.ds(t * 8, 8)] = value.astype(bf16).reshape(8, PIECE, BLOCK)

    def column_in_root():
        return send(column.at[0], column_in.at[s], column_s, column_r, (ROOT, r))

    def column_out(d):
        return send(column.at[1], column_in.at[ROOT], column_s, column_r, ((ROOT + d) % COLS, r))

    def hold_first(d):
        return send(ready.at[0, peer(d)], held_first.at[r], held_s.at[0], held_r.at[TURNS], other(d))

    def hold_second(turn, d):
        return send(ready.at[1, peer(d), :, pl.ds(turn * BACK, BACK)], held[turn].at[r],
                    held_s.at[1], held_r.at[turn], other(d))

    def start_second(turn):
        @pl.loop(1, REPS)
        def _(d):
            hold_second(turn, d).start()

        held[turn][r] = ready[1, r, :, pl.ds(turn * BACK, BACK)]

    def graft(k):
        def square_sum(i, carry):
            value, power = carry
            p = precond[k, pl.ds(pl.multiple_of(i * PIECE, PIECE), PIECE), :]
            g = block_in[k, i].astype(f32)
            return value + g * g, power + p * p

        zero = jnp.zeros((PIECE, BLOCK), f32)
        value, power = lax.fori_loop(0, REPS, square_sum, (zero, zero))
        value = jnp.sum(value, axis=(0, 1), keepdims=True) / (BLOCK * BLOCK)
        power = jnp.sum(power, axis=(0, 1), keepdims=True) / (BLOCK * BLOCK)
        scale = jnp.sqrt(value + epsilon) / jnp.sqrt(power + epsilon)
        scale_own[pl.ds(k, 1), :] = jnp.broadcast_to(scale, (1, 128))

    def scale_send(d):
        return send(scale_own, scale_in.at[r], scale_s, scale_r, other(d))

    wait_first(0)
    wait_first(1)
    product(0, 0, 2 * WIDE)
    wait_first(2)
    product(0, 2 * WIDE, WIDE)
    wait_second(0)
    product(1, 0, BACK)
    wait_first(3)
    landed(squares_in.at[pl.ds(1, REPS - 1)], square_r)
    column[0] = lax.fori_loop(1, REPS, lambda d, value: value + squares_in[d], squares_in[0])

    @pl.when(s != ROOT)
    def _():
        column_in_root().start()

    product(0, 3 * WIDE, WIDE)

    @pl.loop(1, REPS)
    def _(d):
        hold_first(d).start()

    held_first[r] = ready[0, r]
    graft(0)

    wait_second(1)
    product(1, BACK, BACK)
    start_second(0)
    graft(1)

    @pl.loop(1, REPS)
    def _(d):
        scale_send(d).start()

    scale_in[r] = scale_own[...]
    for turn in range(1, TURNS):
        start_second(turn)

    @pl.when(s == ROOT)
    def _():
        landed(column_in.at[pl.ds(0, COLS - 1)], column_r)

        def gather(d, value):
            return value + column_in[(ROOT + d) % COLS]

        column[1] = lax.fori_loop(1, COLS, gather, column[0])
        column_in[ROOT] = column[1]

        @pl.loop(1, COLS)
        def _(d):
            column_out(d).start()

    for copy in stats:
        copy.wait()

    @pl.loop(0, SLOTS)
    def _(k):
        filled = table[0, r * SLOTS + k] < REPS
        keep = jnp.where(filled, decay_keep, 1.0).astype(f32)
        weight = (1.0 - decay_keep) / BLOCK
        for t in range(2):
            rows = pl.ds(t * 256, 256)
            block = block_in[k].reshape(BLOCK, BLOCK)
            left = lax.dot_general(
                block[t * 256:(t + 1) * 256], block, (((1,), (1,)), ((), ())),
                preferred_element_type=f32)
            left_out[k, rows, :] = keep * stat_in[0, k, rows, :] + weight * left
            right = lax.dot_general(
                block[:, t * 256:(t + 1) * 256], block, (((0,), (0,)), ((), ())),
                preferred_element_type=f32)
            right_out[k, rows, :] = keep * stat_in[1, k, rows, :] + weight * right

    @pl.when(s != ROOT)
    def _():
        landed(column_in.at[ROOT], column_r)

    rms = jnp.sqrt(jnp.sum(column_in[ROOT], axis=(0, 1), keepdims=True)
                   / (COLS * REPS * BLOCK * BLOCK))
    clip = jnp.minimum(1.0, rms_limit / rms)

    landed(scale_in.at[pl.ds(0, REPS - 1)], scale_r)

    def settle(turn, d):
        return send(to_place.at[turn, peer(d)], update.at[r, :, pl.ds(turn * BACK, BACK)],
                    place_s, place_r, other(d))

    for turn in range(TURNS):
        if turn == 0:
            landed(held_first.at[pl.ds(0, REPS - 1)], held_r.at[TURNS])
        landed(held[turn].at[pl.ds(0, REPS - 1)], held_r.at[turn])

        @pl.loop(0, REPS)
        def _(j):
            o, k = table[1, j], table[2, j]
            scales = scale_in[o]
            scale = jnp.where(k == 0, scales[:1], scales[1:]) * clip
            value = jnp.where(k == 0, held_first[o, :, pl.ds(turn * BACK, BACK)], held[turn][o])
            value = value.astype(f32)
            for part in range(BACK // 128):
                to_place[turn, j, :, pl.ds(part * 128, 128)] = (
                    value[:, part * 128:(part + 1) * 128] * scale).astype(bf16)

        @pl.loop(1, REPS)
        def _(d):
            settle(turn, d).start()

        update[r, :, pl.ds(turn * BACK, BACK)] = to_place[turn, r]

    left(far_in, far_s)
    left(near_own, near_s)
    left(near_own, both_s)
    left(line_far, lfar_s)
    left(line_far, lnear_s)
    left(line_far, lboth_s)
    left(line_in, line_s)
    left(to_first.at[:, pl.ds(0, REPS - 1)], owner_s.at[0])
    left(to_second.at[:, pl.ds(0, REPS - 1)], owner_s.at[1])
    left(ready.at[0, pl.ds(0, REPS - 1)], held_s.at[0])
    left(ready.at[1, pl.ds(0, REPS - 1)], held_s.at[1])
    left(to_place.at[:, pl.ds(0, REPS - 1)], place_s)
    left(squares_in.at[pl.ds(1, REPS - 1)], square_s)
    left(scale_in.at[pl.ds(0, REPS - 1)], scale_s)

    @pl.when(s != ROOT)
    def _():
        left(column_in.at[ROOT], column_s)

    @pl.when(s == ROOT)
    def _():
        left(column_in.at[pl.ds(0, COLS - 1)], column_s)

    landed(update.at[pl.ds(0, REPS - 1)], place_r)


def on_device(partial_grads, owner_list, left_stat, right_stat, left_root, right_root):
    grads = partial_grads.reshape(REPS, SIDE, SIDE, 2, HALF, BLOCK)
    hbm_spec = pl.BlockSpec(memory_space=pltpu.HBM)
    vmem_spec = pl.BlockSpec(memory_space=pltpu.VMEM)
    dma = pltpu.SemaphoreType.DMA
    groups = 2 * STEPS
    lines = groups - 2
    quarter = (2, 8, SIDE, HALF, WIDE)
    eighth = (2, 8, HALF, WIDE)
    state = pltpu.VMEM((SLOTS, BLOCK, BLOCK), f32)
    update, left_new, right_new = pl.pallas_call(
        kernel,
        out_shape=(pltpu.VMEM((REPS, PIECE, BLOCK), bf16), state, state),
        in_specs=[hbm_spec] * 6,
        out_specs=(vmem_spec, vmem_spec, vmem_spec),
        scratch_shapes=[
            pltpu.VMEM((groups,) + quarter, bf16),
            pltpu.VMEM((groups, 2) + quarter, bf16),
            pltpu.VMEM((groups,) + quarter, bf16),
            pltpu.VMEM((groups, REPS, SIDE, HALF, WIDE), bf16),
            pltpu.VMEM((groups, SIDE, REPS, HALF, WIDE), bf16),
            pltpu.VMEM((lines,) + eighth, bf16),
            pltpu.VMEM((lines, 2) + eighth, bf16),
            pltpu.VMEM((2, 3, REPS, HALF, WIDE), bf16),
            pltpu.VMEM((STEPS, REPS + 1, PIECE, WIDE), bf16),
            pltpu.VMEM((STEPS, REPS, PIECE, WIDE), bf16),
            pltpu.VMEM((TURNS, REPS, PIECE, BACK), bf16),
            pltpu.VMEM((SLOTS, REPS, PIECE, BLOCK), bf16),
            pltpu.VMEM((2, SLOTS, BLOCK, BLOCK), f32),
            pltpu.VMEM((2, SLOTS, BLOCK, BLOCK), bf16),
            pltpu.VMEM((2, SLOTS, BLOCK, BLOCK), bf16),
            pltpu.VMEM((2, SLOTS, BLOCK, BLOCK), f32),
            pltpu.VMEM((SLOTS, BLOCK, BLOCK), f32),
            pltpu.VMEM((SLOTS, REPS, PIECE, BLOCK), bf16),
            pltpu.VMEM((REPS, PIECE, BLOCK), bf16),
            pltpu.VMEM((REPS, PIECE, BACK), bf16),
            pltpu.VMEM((REPS, PIECE, BACK), bf16),
            pltpu.VMEM((SLOTS, 128), f32),
            pltpu.VMEM((REPS, SLOTS, 128), f32),
            pltpu.VMEM((TURNS, REPS, PIECE, BACK), bf16),
            pltpu.VMEM((8, 128), f32),
            pltpu.VMEM((REPS, 1, 128), f32),
            pltpu.VMEM((2, 1, 128), f32),
            pltpu.VMEM((COLS, 1, 128), f32),
            pltpu.SMEM((1, COLS * REPS), jnp.int32),
            pltpu.SMEM((3, REPS * SLOTS), jnp.int32),
            dma((STEPS,)), dma((STEPS,)), dma((2,)), dma((2,)), dma,
            dma, dma((STEPS,)), dma, dma, dma((STEPS,)),
            dma, dma((STEPS - 1,)), dma, dma, dma((STEPS - 1,)),
            dma, dma, dma((2,)), dma((STEPS + TURNS,)),
            dma((2,)), dma((TURNS + 1,)), dma, dma, dma, dma,
            dma, dma, dma, dma,
        ],
        compiler_params=pltpu.CompilerParams(
            collective_id=0, has_side_effects=True, vmem_limit_bytes=58 << 20),
    )(grads, owner_list.reshape(1, COLS * REPS),
      left_stat[0, 0], right_stat[0, 0], left_root[0, 0], right_root[0, 0])
    return (update.reshape(1, BLOCK, BLOCK), left_new[None, None], right_new[None, None])


def solution(mesh):
    return jax.shard_map(
        on_device,
        mesh=mesh,
        in_specs=(
            P("replica", "shard", None, None),
            P(),
            P("shard", "replica", None, None, None),
            P("shard", "replica", None, None, None),
            P("shard", "replica", None, None, None),
            P("shard", "replica", None, None, None),
        ),
        out_specs=(
            P(("shard", "replica"), None, None),
            P("shard", "replica", None, None, None),
            P("shard", "replica", None, None, None),
        ),
        check_vma=False,
    )
```

```python
import functools

import jax
import jax.numpy as jnp
from jax import lax
from jax.experimental import pallas as pl
from jax.experimental.pallas import tpu as pltpu
from jax.sharding import PartitionSpec as P

decay_keep = 0.9
epsilon = 1e-06
rms_limit = 0.5

MESH = pl.DeviceIdType.MESH
f32 = jnp.float32
bf16 = jnp.bfloat16

SIDE = 4
REPS = 16
COLS = 8
ROOT = 1
SLOTS = 2
BLOCK = 512
PIECE = 32
HALF = 16
WIDE = 128
STEPS = BLOCK // WIDE
BACK = 256
TURNS = BLOCK // BACK


def kernel(
    grads, owner_list, left_stat, right_stat, left_root, right_root,
    update, left_out, right_out,
    far_in, pass_in, near_own, last_own,
    line_sum, line_far, line_pass, line_in, piece,
    to_first, to_second, block_in, root_in, root_hi, root_lo, stat_in, precond, ready,
    held_first, held_0, held_1, scale_own, scale_in, to_place,
    squares, squares_in, column, column_in, owners, table,
    near_sem, last_sem, root_sem, stat_sem, list_sem,
    far_s, far_r, near_s, both_s, pass_r, lfar_s, lfar_r, lnear_s, lboth_s, lpass_r,
    line_s, line_r, owner_s, owner_r, held_s, held_r, scale_s, scale_r, place_s, place_r,
    square_s, square_r, column_s, column_r,
):
    s = lax.axis_index("shard")
    r = lax.axis_index("replica")
    x, y = r % SIDE, r // SIDE
    held = (held_0, held_1)

    def along(half, step):
        if half == 0:
            return (s, y * SIDE + (x + step) % SIDE)
        return (s, (y + step) % SIDE * SIDE + x)

    def peer(d):
        turned = d * 7 % REPS
        return (y + turned // SIDE) % SIDE * SIDE + (x + turned % SIDE) % SIDE

    def other(d):
        return (s, peer(d))

    def send(src, dst, send_sem, recv_sem, device):
        return pltpu.make_async_remote_copy(
            src_ref=src, dst_ref=dst, send_sem=send_sem, recv_sem=recv_sem,
            device_id=device, device_id_type=MESH,
        )

    def landed(ref, sem):
        send(ref, ref, column_s, sem, other(1)).wait_recv()

    def left(ref, sem):
        send(ref, ref, sem, column_r, other(1)).wait_send()

    def loaded(ref, sem):
        pltpu.make_async_copy(ref, ref, sem).wait()

    barrier = pltpu.get_barrier_semaphore()
    for half in range(2):
        for step in (1, 3):
            pl.semaphore_signal(barrier, inc=1, device_id=along(half, step), device_id_type=MESH)

    @pl.when(s == ROOT)
    def _():
        @pl.loop(1, COLS)
        def _(d):
            pl.semaphore_signal(barrier, inc=1, device_id=((s + d) % COLS, r), device_id_type=MESH)

        pl.semaphore_wait(barrier, 4)

    @pl.when(s != ROOT)
    def _():
        pl.semaphore_wait(barrier, 5)

    def chunk(g, step, first, count):
        wide, half = g // 2, g % 2
        place = ((x if half == 0 else y) + step) % SIDE
        rows = pl.ds(first, count)
        cols = pl.ds(wide * WIDE, WIDE)
        if half == 0:
            return grads.at[rows, :, place, 0, :, cols]
        return grads.at[rows, place, :, 1, :, cols]

    def far(g, way):
        return send(chunk(g, 2, 8 * way, 8), far_in.at[g, way],
                    far_s, far_r.at[g // 2], along(g % 2, 1 - 2 * way))

    def near(g, way):
        return send(chunk(g, 1 - 2 * way, 8 - 8 * way, 8), pass_in.at[g, 0, way],
                    near_s, pass_r.at[g // 2], along(g % 2, 1 - 2 * way))

    def both(g, way):
        return send(near_own.at[g, way], pass_in.at[g, 1, way],
                    both_s, pass_r.at[g // 2], along(g % 2, 1 - 2 * way))

    def load_near(g, way):
        return pltpu.make_async_copy(chunk(g, 1 - 2 * way, 8 * way, 8),
                                     near_own.at[g, way], near_sem.at[g // 2])

    def load_last(g):
        return pltpu.make_async_copy(chunk(g, 0, 0, REPS), last_own.at[g], last_sem.at[g // 2])

    def line_place(g, step):
        return ((y if g % 2 == 0 else x) + step) % SIDE

    def line(g, d):
        return send(line_sum.at[g, line_place(g, d)], line_in.at[g % 2, d - 1],
                    line_s, line_r, along(1 - g % 2, d))

    def lfar(g, way):
        return send(line_sum.at[g, line_place(g, 2), pl.ds(8 * way, 8)], line_far.at[g, way],
                    lfar_s, lfar_r.at[g // 2], along(1 - g % 2, 1 - 2 * way))

    def lnear(g, way):
        return send(line_sum.at[g, line_place(g, 1 - 2 * way), pl.ds(8 - 8 * way, 8)],
                    line_pass.at[g, 0, way],
                    lnear_s, lpass_r.at[g // 2], along(1 - g % 2, 1 - 2 * way))

    def lboth(g, way):
        return send(line_sum.at[g, line_place(g, 1 - 2 * way), pl.ds(8 * way, 8)],
                    line_pass.at[g, 1, way],
                    lboth_s, lpass_r.at[g // 2], along(1 - g % 2, 1 - 2 * way))

    def pair(wide):
        return pl.ds(2 * wide, 2)

    def direct(wide):
        return wide == STEPS - 1

    def start_far(wide):
        for g in (2 * wide, 2 * wide + 1):
            for way in range(2):
                far(g, way).start()
                load_near(g, way).start()

    def start_near(wide):
        for g in (2 * wide, 2 * wide + 1):
            for way in range(2):
                near(g, way).start()
            load_last(g).start()

    def combine(wide):
        loaded(near_own.at[pair(wide)], near_sem.at[wide])
        landed(far_in.at[pair(wide)], far_r.at[wide])
        for g in (2 * wide, 2 * wide + 1):
            for way in range(2):
                @pl.loop(0, 8)
                def _(b):
                    near_own[g, way, b] = near_own[g, way, b] + far_in[g, way, b]

                both(g, way).start()

    def line_total(wide):
        loaded(last_own.at[pair(wide)], last_sem.at[wide])
        landed(pass_in.at[pair(wide)], pass_r.at[wide])
        for g in (2 * wide, 2 * wide + 1):
            @pl.loop(0, 8)
            def _(b):
                for way in range(2):
                    total = (last_own[g, 8 * way + b].astype(f32)
                             + pass_in[g, 1, way, b].astype(f32)
                             + pass_in[g, 0, 1 - way, b].astype(f32))
                    line_sum[g, :, 8 * way + b] = total.astype(bf16)

            if direct(wide):
                for d in (2, 1, 3):
                    line(g, d).start()
            else:
                for way in range(2):
                    lfar(g, way).start()
                for way in range(2):
                    lnear(g, way).start()

    def line_combine(wide):
        landed(line_far.at[pair(wide)], lfar_r.at[wide])
        for g in (2 * wide, 2 * wide + 1):
            for way in range(2):
                place = line_place(g, 1 - 2 * way)

                @pl.loop(0, 8)
                def _(b):
                    line_sum[g, place, 8 * way + b] = (
                        line_sum[g, place, 8 * way + b] + line_far[g, way, b])

                lboth(g, way).start()

    def total(wide):
        if direct(wide):
            landed(line_in, line_r)
        else:
            landed(line_pass.at[pair(wide)], lpass_r.at[wide])
        for g in (2 * wide, 2 * wide + 1):
            place = line_place(g, 0)

            def finish(b, value):
                value = value.astype(bf16)
                piece[wide, b, pl.ds(g % 2 * HALF, HALF), :] = value
                value = value.astype(f32)
                value = value * value
                squares[...] += value[:8] + value[8:]

            if direct(wide):
                @pl.loop(0, REPS)
                def _(b):
                    value = line_sum[g, place, b].astype(f32)
                    for d in range(3):
                        value = value + line_in[g % 2, d, b].astype(f32)
                    finish(b, value)
            else:
                @pl.loop(0, 8)
                def _(b):
                    for way in range(2):
                        finish(8 * way + b,
                               line_sum[g, place, 8 * way + b].astype(f32)
                               + line_pass[g, 1, way, b].astype(f32)
                               + line_pass[g, 0, 1 - way, b].astype(f32))

    def columns(wide):
        return pl.ds(wide * WIDE, WIDE)

    def owner_first(wide, d):
        return send(to_first.at[wide, peer(d)], block_in.at[0, r, :, columns(wide)],
                    owner_s.at[0], owner_r.at[wide], other(d))

    def owner_second(turn, d):
        return send(to_second.at[turn, peer(d)], block_in.at[1, r, :, pl.ds(turn * BACK, BACK)],
                    owner_s.at[1], owner_r.at[STEPS + turn], other(d))

    def route_first(wide):
        @pl.loop(0, REPS)
        def _(o):
            to_first[wide, o] = piece[wide, table[0, o * SLOTS]]

        @pl.loop(1, REPS)
        def _(d):
            owner_first(wide, d).start()

        block_in[0, r, :, columns(wide)] = to_first[wide, r]

    def route_second(turn):
        each = BACK // WIDE

        @pl.loop(0, REPS)
        def _(o):
            for i in range(each):
                to_second[turn, o, :, pl.ds(i * WIDE, WIDE)] = (
                    piece[turn * each + i, table[0, o * SLOTS + 1]])

        @pl.loop(1, REPS)
        def _(d):
            owner_second(turn, d).start()

        block_in[1, r, :, pl.ds(turn * BACK, BACK)] = to_second[turn, r]

    def wait_first(wide):
        landed(block_in.at[0, pl.ds(0, REPS - 1), :, columns(wide)], owner_r.at[wide])

    def wait_second(turn):
        landed(block_in.at[1, pl.ds(0, REPS - 1), :, pl.ds(turn * BACK, BACK)],
               owner_r.at[STEPS + turn])

    roots = [pltpu.make_async_copy(ref, root_in.at[i], root_sem.at[i])
             for i, ref in enumerate((left_root, right_root))]
    stats = [pltpu.make_async_copy(ref, stat_in.at[i], stat_sem.at[i])
             for i, ref in enumerate((left_stat, right_stat))]

    names = pltpu.make_async_copy(owner_list, owners, list_sem)

    start_far(0)
    names.start()
    start_near(0)
    start_far(1)
    for copy in roots:
        copy.start()

    names.wait()

    @pl.loop(0, REPS)
    def _(j):
        mine = owners[0, s * REPS + j]
        count = jnp.int32(0)
        for i in range(REPS):
            hit = (owners[0, s * REPS + i] == mine) & (i < j)
            count = count + hit.astype(jnp.int32)
        table[1, j] = mine
        table[2, j] = jnp.minimum(count, SLOTS - 1)

    @pl.loop(0, REPS)
    def _(o):
        first, second = jnp.int32(REPS), jnp.int32(REPS)
        for j in range(REPS):
            hit = table[1, j] == o
            first = jnp.where(hit & (table[2, j] == 0), j, first)
            second = jnp.where(hit & (table[2, j] == 1), j, second)
        table[0, o * SLOTS] = first
        table[0, o * SLOTS + 1] = second

    for wide in range(STEPS):
        piece[wide, REPS] = jnp.zeros((PIECE, WIDE), bf16)
    squares[...] = jnp.zeros_like(squares)

    def split(side):
        roots[side].wait()

        @pl.loop(0, SLOTS * 8)
        def _(i):
            k, t = i // 8, i % 8
            rows = pl.ds(pl.multiple_of(t * 64, 64), 64)
            whole = root_in[side, k, rows, :]
            top = whole.astype(bf16)
            root_hi[side, k, rows, :] = top
            root_lo[side, k, rows, :] = (whole - top.astype(f32)).astype(bf16)

    combine(0)
    start_near(1)
    start_far(2)
    start_far(3)
    for side in range(2):
        split(side)
    for wide in range(STEPS):
        if wide + 1 < STEPS:
            combine(wide + 1)
        if wide + 2 < STEPS:
            start_near(wide + 2)
        if wide >= 1 and not direct(wide):
            line_combine(wide - 1)
        line_total(wide)
        if direct(wide):
            line_combine(wide - 1)
        if wide == 0:
            for copy in stats:
                copy.start()
        if wide >= 1:
            total(wide - 1)
        if wide >= 2:
            route_first(wide - 2)
    route_first(STEPS - 2)
    route_second(0)
    total(STEPS - 1)
    route_first(STEPS - 1)

    def square(d):
        return send(squares_in.at[0], squares_in.at[d], square_s, square_r, other(d))

    squares_in[0] = jnp.sum(squares[...], axis=0, keepdims=True)

    @pl.loop(1, REPS)
    def _(d):
        square(d).start()

    route_second(1)


    def product(k, first, count):
        @pl.loop(0, 2)
        def _(t):
            rows = pl.ds(pl.multiple_of(t * 256, 256), 256)
            across = pl.ds(first, count)
            block = block_in[k, :, :, across].reshape(BLOCK, count)
            part = (jnp.dot(root_hi[0, k, rows, :], block, preferred_element_type=f32)
                    + jnp.dot(root_lo[0, k, rows, :], block, preferred_element_type=f32))
            top = part.astype(bf16)
            low = (part - top.astype(f32)).astype(bf16)
            hi, lo = root_hi[1, k, across, :], root_lo[1, k, across, :]
            value = (jnp.dot(top, hi, preferred_element_type=f32)
                     + jnp.dot(top, lo, preferred_element_type=f32)
                     + jnp.dot(low, hi, preferred_element_type=f32))
            if first > 0:
                value = precond[k, rows, :] + value
            precond[k, rows, :] = value
            if first + count == BLOCK:
                ready[k, pl.ds(t * 8, 8)] = value.astype(bf16).reshape(8, PIECE, BLOCK)

    def column_in_root():
        return send(column.at[0], column_in.at[s], column_s, column_r, (ROOT, r))

    def column_out(d):
        return send(column.at[1], column_in.at[ROOT], column_s, column_r, ((ROOT + d) % COLS, r))

    def hold_first(d):
        return send(ready.at[0, peer(d)], held_first.at[r], held_s.at[0], held_r.at[TURNS], other(d))

    def hold_second(turn, d):
        return send(ready.at[1, peer(d), :, pl.ds(turn * BACK, BACK)], held[turn].at[r],
                    held_s.at[1], held_r.at[turn], other(d))

    def start_second(turn):
        @pl.loop(1, REPS)
        def _(d):
            hold_second(turn, d).start()

        held[turn][r] = ready[1, r, :, pl.ds(turn * BACK, BACK)]

    def graft(k):
        def square_sum(i, carry):
            value, power = carry
            p = precond[k, pl.ds(pl.multiple_of(i * PIECE, PIECE), PIECE), :]
            g = block_in[k, i].astype(f32)
            return value + g * g, power + p * p

        zero = jnp.zeros((PIECE, BLOCK), f32)
        value, power = lax.fori_loop(0, REPS, square_sum, (zero, zero))
        value = jnp.sum(value, axis=(0, 1), keepdims=True) / (BLOCK * BLOCK)
        power = jnp.sum(power, axis=(0, 1), keepdims=True) / (BLOCK * BLOCK)
        scale = jnp.sqrt(value + epsilon) / jnp.sqrt(power + epsilon)
        scale_own[pl.ds(k, 1), :] = jnp.broadcast_to(scale, (1, 128))

    def scale_send(d):
        return send(scale_own, scale_in.at[r], scale_s, scale_r, other(d))

    wait_first(0)
    wait_first(1)
    product(0, 0, 2 * WIDE)
    wait_first(2)
    product(0, 2 * WIDE, WIDE)
    wait_first(3)
    landed(squares_in.at[pl.ds(1, REPS - 1)], square_r)
    column[0] = lax.fori_loop(1, REPS, lambda d, value: value + squares_in[d], squares_in[0])

    @pl.when(s != ROOT)
    def _():
        column_in_root().start()

    product(0, 3 * WIDE, WIDE)

    @pl.loop(1, REPS)
    def _(d):
        hold_first(d).start()

    held_first[r] = ready[0, r]
    wait_second(0)
    product(1, 0, BACK)
    wait_second(1)
    product(1, BACK, BACK)
    start_second(0)
    graft(0)
    graft(1)

    @pl.loop(1, REPS)
    def _(d):
        scale_send(d).start()

    scale_in[r] = scale_own[...]
    for turn in range(1, TURNS):
        start_second(turn)

    @pl.when(s == ROOT)
    def _():
        landed(column_in.at[pl.ds(0, COLS - 1)], column_r)

        def gather(d, value):
            return value + column_in[(ROOT + d) % COLS]

        column[1] = lax.fori_loop(1, COLS, gather, column[0])
        column_in[ROOT] = column[1]

        @pl.loop(1, COLS)
        def _(d):
            column_out(d).start()

    for copy in stats:
        copy.wait()

    @pl.loop(0, SLOTS)
    def _(k):
        filled = table[0, r * SLOTS + k] < REPS
        keep = jnp.where(filled, decay_keep, 1.0).astype(f32)
        weight = (1.0 - decay_keep) / BLOCK
        for t in range(2):
            rows = pl.ds(t * 256, 256)
            block = block_in[k].reshape(BLOCK, BLOCK)
            left = lax.dot_general(
                block[t * 256:(t + 1) * 256], block, (((1,), (1,)), ((), ())),
                preferred_element_type=f32)
            left_out[k, rows, :] = keep * stat_in[0, k, rows, :] + weight * left
            right = lax.dot_general(
                block[:, t * 256:(t + 1) * 256], block, (((0,), (0,)), ((), ())),
                preferred_element_type=f32)
            right_out[k, rows, :] = keep * stat_in[1, k, rows, :] + weight * right

    @pl.when(s != ROOT)
    def _():
        landed(column_in.at[ROOT], column_r)

    rms = jnp.sqrt(jnp.sum(column_in[ROOT], axis=(0, 1), keepdims=True)
                   / (COLS * REPS * BLOCK * BLOCK))
    clip = jnp.minimum(1.0, rms_limit / rms)

    landed(scale_in.at[pl.ds(0, REPS - 1)], scale_r)

    def settle(turn, d):
        return send(to_place.at[turn, peer(d)], update.at[r, :, pl.ds(turn * BACK, BACK)],
                    place_s, place_r, other(d))

    for turn in range(TURNS):
        if turn == 0:
            landed(held_first.at[pl.ds(0, REPS - 1)], held_r.at[TURNS])
        landed(held[turn].at[pl.ds(0, REPS - 1)], held_r.at[turn])

        @pl.loop(0, REPS)
        def _(j):
            o, k = table[1, j], table[2, j]
            scales = scale_in[o]
            scale = jnp.where(k == 0, scales[:1], scales[1:]) * clip
            value = jnp.where(k == 0, held_first[o, :, pl.ds(turn * BACK, BACK)], held[turn][o])
            value = value.astype(f32)
            for part in range(BACK // 128):
                to_place[turn, j, :, pl.ds(part * 128, 128)] = (
                    value[:, part * 128:(part + 1) * 128] * scale).astype(bf16)

        @pl.loop(1, REPS)
        def _(d):
            settle(turn, d).start()

        update[r, :, pl.ds(turn * BACK, BACK)] = to_place[turn, r]

    left(far_in, far_s)
    left(near_own, near_s)
    left(near_own, both_s)
    left(line_far, lfar_s)
    left(line_far, lnear_s)
    left(line_far, lboth_s)
    left(line_in, line_s)
    left(to_first.at[:, pl.ds(0, REPS - 1)], owner_s.at[0])
    left(to_second.at[:, pl.ds(0, REPS - 1)], owner_s.at[1])
    left(ready.at[0, pl.ds(0, REPS - 1)], held_s.at[0])
    left(ready.at[1, pl.ds(0, REPS - 1)], held_s.at[1])
    left(to_place.at[:, pl.ds(0, REPS - 1)], place_s)
    left(squares_in.at[pl.ds(1, REPS - 1)], square_s)
    left(scale_in.at[pl.ds(0, REPS - 1)], scale_s)

    @pl.when(s != ROOT)
    def _():
        left(column_in.at[ROOT], column_s)

    @pl.when(s == ROOT)
    def _():
        left(column_in.at[pl.ds(0, COLS - 1)], column_s)

    landed(update.at[pl.ds(0, REPS - 1)], place_r)


def on_device(partial_grads, owner_list, left_stat, right_stat, left_root, right_root):
    grads = partial_grads.reshape(REPS, SIDE, SIDE, 2, HALF, BLOCK)
    hbm_spec = pl.BlockSpec(memory_space=pltpu.HBM)
    vmem_spec = pl.BlockSpec(memory_space=pltpu.VMEM)
    dma = pltpu.SemaphoreType.DMA
    groups = 2 * STEPS
    lines = groups - 2
    quarter = (2, 8, SIDE, HALF, WIDE)
    eighth = (2, 8, HALF, WIDE)
    state = pltpu.VMEM((SLOTS, BLOCK, BLOCK), f32)
    update, left_new, right_new = pl.pallas_call(
        kernel,
        out_shape=(pltpu.VMEM((REPS, PIECE, BLOCK), bf16), state, state),
        in_specs=[hbm_spec] * 6,
        out_specs=(vmem_spec, vmem_spec, vmem_spec),
        scratch_shapes=[
            pltpu.VMEM((groups,) + quarter, bf16),
            pltpu.VMEM((groups, 2) + quarter, bf16),
            pltpu.VMEM((groups,) + quarter, bf16),
            pltpu.VMEM((groups, REPS, SIDE, HALF, WIDE), bf16),
            pltpu.VMEM((groups, SIDE, REPS, HALF, WIDE), bf16),
            pltpu.VMEM((lines,) + eighth, bf16),
            pltpu.VMEM((lines, 2) + eighth, bf16),
            pltpu.VMEM((2, 3, REPS, HALF, WIDE), bf16),
            pltpu.VMEM((STEPS, REPS + 1, PIECE, WIDE), bf16),
            pltpu.VMEM((STEPS, REPS, PIECE, WIDE), bf16),
            pltpu.VMEM((TURNS, REPS, PIECE, BACK), bf16),
            pltpu.VMEM((SLOTS, REPS, PIECE, BLOCK), bf16),
            pltpu.VMEM((2, SLOTS, BLOCK, BLOCK), f32),
            pltpu.VMEM((2, SLOTS, BLOCK, BLOCK), bf16),
            pltpu.VMEM((2, SLOTS, BLOCK, BLOCK), bf16),
            pltpu.VMEM((2, SLOTS, BLOCK, BLOCK), f32),
            pltpu.VMEM((SLOTS, BLOCK, BLOCK), f32),
            pltpu.VMEM((SLOTS, REPS, PIECE, BLOCK), bf16),
            pltpu.VMEM((REPS, PIECE, BLOCK), bf16),
            pltpu.VMEM((REPS, PIECE, BACK), bf16),
            pltpu.VMEM((REPS, PIECE, BACK), bf16),
            pltpu.VMEM((SLOTS, 128), f32),
            pltpu.VMEM((REPS, SLOTS, 128), f32),
            pltpu.VMEM((TURNS, REPS, PIECE, BACK), bf16),
            pltpu.VMEM((8, 128), f32),
            pltpu.VMEM((REPS, 1, 128), f32),
            pltpu.VMEM((2, 1, 128), f32),
            pltpu.VMEM((COLS, 1, 128), f32),
            pltpu.SMEM((1, COLS * REPS), jnp.int32),
            pltpu.SMEM((3, REPS * SLOTS), jnp.int32),
            dma((STEPS,)), dma((STEPS,)), dma((2,)), dma((2,)), dma,
            dma, dma((STEPS,)), dma, dma, dma((STEPS,)),
            dma, dma((STEPS - 1,)), dma, dma, dma((STEPS - 1,)),
            dma, dma, dma((2,)), dma((STEPS + TURNS,)),
            dma((2,)), dma((TURNS + 1,)), dma, dma, dma, dma,
            dma, dma, dma, dma,
        ],
        compiler_params=pltpu.CompilerParams(
            collective_id=0, has_side_effects=True, vmem_limit_bytes=58 << 20),
    )(grads, owner_list.reshape(1, COLS * REPS),
      left_stat[0, 0], right_stat[0, 0], left_root[0, 0], right_root[0, 0])
    return (update.reshape(1, BLOCK, BLOCK), left_new[None, None], right_new[None, None])


def solution(mesh):
    return jax.shard_map(
        on_device,
        mesh=mesh,
        in_specs=(
            P("replica", "shard", None, None),
            P(),
            P("shard", "replica", None, None, None),
            P("shard", "replica", None, None, None),
            P("shard", "replica", None, None, None),
            P("shard", "replica", None, None, None),
        ),
        out_specs=(
            P(("shard", "replica"), None, None),
            P("shard", "replica", None, None, None),
            P("shard", "replica", None, None, None),
        ),
        check_vma=False,
    )
```

```python
import functools

import jax
import jax.numpy as jnp
from jax import lax
from jax.experimental import pallas as pl
from jax.experimental.pallas import tpu as pltpu
from jax.sharding import PartitionSpec as P

decay_keep = 0.9
epsilon = 1e-06
rms_limit = 0.5

MESH = pl.DeviceIdType.MESH
f32 = jnp.float32
bf16 = jnp.bfloat16

SIDE = 4
REPS = 16
COLS = 8
ROOT = 1
SLOTS = 2
BLOCK = 512
PIECE = 32
HALF = 16
WIDE = 128
STEPS = BLOCK // WIDE
BACK = 256
TURNS = BLOCK // BACK


def kernel(
    grads, owner_list, left_stat, right_stat, left_root, right_root,
    update, left_out, right_out,
    far_in, pass_in, near_own, last_own,
    line_sum, line_far, line_pass, line_in, piece,
    to_first, to_second, block_in, root_in, root_hi, root_lo, stat_in, precond, ready,
    held_first, held_0, held_1, scale_own, scale_in, to_place,
    squares, squares_in, column, column_in, owners, table,
    near_sem, last_sem, root_sem, stat_sem, list_sem,
    far_s, far_r, near_s, both_s, pass_r, lfar_s, lfar_r, lnear_s, lboth_s, lpass_r,
    line_s, line_r, owner_s, owner_r, held_s, held_r, scale_s, scale_r, place_s, place_r,
    square_s, square_r, column_s, column_r,
):
    s = lax.axis_index("shard")
    r = lax.axis_index("replica")
    x, y = r % SIDE, r // SIDE
    held = (held_0, held_1)

    def along(half, step):
        if half == 0:
            return (s, y * SIDE + (x + step) % SIDE)
        return (s, (y + step) % SIDE * SIDE + x)

    def peer(d):
        turned = d * 7 % REPS
        return (y + turned // SIDE) % SIDE * SIDE + (x + turned % SIDE) % SIDE

    def other(d):
        return (s, peer(d))

    def send(src, dst, send_sem, recv_sem, device):
        return pltpu.make_async_remote_copy(
            src_ref=src, dst_ref=dst, send_sem=send_sem, recv_sem=recv_sem,
            device_id=device, device_id_type=MESH,
        )

    def landed(ref, sem):
        send(ref, ref, column_s, sem, other(1)).wait_recv()

    def left(ref, sem):
        send(ref, ref, sem, column_r, other(1)).wait_send()

    def loaded(ref, sem):
        pltpu.make_async_copy(ref, ref, sem).wait()

    barrier = pltpu.get_barrier_semaphore()
    for half in range(2):
        for step in (1, 3):
            pl.semaphore_signal(barrier, inc=1, device_id=along(half, step), device_id_type=MESH)

    @pl.when(s == ROOT)
    def _():
        @pl.loop(1, COLS)
        def _(d):
            pl.semaphore_signal(barrier, inc=1, device_id=((s + d) % COLS, r), device_id_type=MESH)

        pl.semaphore_wait(barrier, 4)

    @pl.when(s != ROOT)
    def _():
        pl.semaphore_wait(barrier, 5)

    def chunk(g, step, first, count):
        wide, half = g // 2, g % 2
        place = ((x if half == 0 else y) + step) % SIDE
        rows = pl.ds(first, count)
        cols = pl.ds(wide * WIDE, WIDE)
        if half == 0:
            return grads.at[rows, :, place, 0, :, cols]
        return grads.at[rows, place, :, 1, :, cols]

    def far(g, way):
        return send(chunk(g, 2, 8 * way, 8), far_in.at[g, way],
                    far_s, far_r.at[g // 2], along(g % 2, 1 - 2 * way))

    def near(g, way):
        return send(chunk(g, 1 - 2 * way, 8 - 8 * way, 8), pass_in.at[g, 0, way],
                    near_s, pass_r.at[g // 2], along(g % 2, 1 - 2 * way))

    def both(g, way):
        return send(near_own.at[g, way], pass_in.at[g, 1, way],
                    both_s, pass_r.at[g // 2], along(g % 2, 1 - 2 * way))

    def load_near(g, way):
        return pltpu.make_async_copy(chunk(g, 1 - 2 * way, 8 * way, 8),
                                     near_own.at[g, way], near_sem.at[g // 2])

    def load_last(g):
        return pltpu.make_async_copy(chunk(g, 0, 0, REPS), last_own.at[g], last_sem.at[g // 2])

    def line_place(g, step):
        return ((y if g % 2 == 0 else x) + step) % SIDE

    def line(g, d):
        return send(line_sum.at[g, line_place(g, d)], line_in.at[g % 2, d - 1],
                    line_s, line_r, along(1 - g % 2, d))

    def lfar(g, way):
        return send(line_sum.at[g, line_place(g, 2), pl.ds(8 * way, 8)], line_far.at[g, way],
                    lfar_s, lfar_r.at[g // 2], along(1 - g % 2, 1 - 2 * way))

    def lnear(g, way):
        return send(line_sum.at[g, line_place(g, 1 - 2 * way), pl.ds(8 - 8 * way, 8)],
                    line_pass.at[g, 0, way],
                    lnear_s, lpass_r.at[g // 2], along(1 - g % 2, 1 - 2 * way))

    def lboth(g, way):
        return send(line_sum.at[g, line_place(g, 1 - 2 * way), pl.ds(8 * way, 8)],
                    line_pass.at[g, 1, way],
                    lboth_s, lpass_r.at[g // 2], along(1 - g % 2, 1 - 2 * way))

    def pair(wide):
        return pl.ds(2 * wide, 2)

    def direct(wide):
        return wide == STEPS - 1

    def start_far(wide):
        for g in (2 * wide, 2 * wide + 1):
            for way in range(2):
                far(g, way).start()
                load_near(g, way).start()

    def start_near(wide):
        for g in (2 * wide, 2 * wide + 1):
            for way in range(2):
                near(g, way).start()
            load_last(g).start()

    def combine(wide):
        loaded(near_own.at[pair(wide)], near_sem.at[wide])
        landed(far_in.at[pair(wide)], far_r.at[wide])
        for g in (2 * wide, 2 * wide + 1):
            for way in range(2):
                @pl.loop(0, 8, unroll=2)
                def _(b):
                    near_own[g, way, b] = near_own[g, way, b] + far_in[g, way, b]

                both(g, way).start()

    def line_total(wide):
        loaded(last_own.at[pair(wide)], last_sem.at[wide])
        landed(pass_in.at[pair(wide)], pass_r.at[wide])
        for g in (2 * wide, 2 * wide + 1):
            @pl.loop(0, 8, unroll=2)
            def _(b):
                for way in range(2):
                    total = (last_own[g, 8 * way + b].astype(f32)
                             + pass_in[g, 1, way, b].astype(f32)
                             + pass_in[g, 0, 1 - way, b].astype(f32))
                    line_sum[g, :, 8 * way + b] = total.astype(bf16)

            if direct(wide):
                for d in (2, 1, 3):
                    line(g, d).start()
            else:
                for way in range(2):
                    lfar(g, way).start()
                for way in range(2):
                    lnear(g, way).start()

    def line_combine(wide):
        landed(line_far.at[pair(wide)], lfar_r.at[wide])
        for g in (2 * wide, 2 * wide + 1):
            for way in range(2):
                place = line_place(g, 1 - 2 * way)

                @pl.loop(0, 8, unroll=2)
                def _(b):
                    line_sum[g, place, 8 * way + b] = (
                        line_sum[g, place, 8 * way + b] + line_far[g, way, b])

                lboth(g, way).start()

    def total(wide):
        if direct(wide):
            landed(line_in, line_r)
        else:
            landed(line_pass.at[pair(wide)], lpass_r.at[wide])
        for g in (2 * wide, 2 * wide + 1):
            place = line_place(g, 0)

            def finish(b, value):
                value = value.astype(bf16)
                piece[wide, b, pl.ds(g % 2 * HALF, HALF), :] = value
                value = value.astype(f32)
                value = value * value
                squares[...] += value[:8] + value[8:]

            if direct(wide):
                @pl.loop(0, REPS, unroll=4)
                def _(b):
                    value = line_sum[g, place, b].astype(f32)
                    for d in range(3):
                        value = value + line_in[g % 2, d, b].astype(f32)
                    finish(b, value)
            else:
                @pl.loop(0, 8, unroll=2)
                def _(b):
                    for way in range(2):
                        finish(8 * way + b,
                               line_sum[g, place, 8 * way + b].astype(f32)
                               + line_pass[g, 1, way, b].astype(f32)
                               + line_pass[g, 0, 1 - way, b].astype(f32))

    def columns(wide):
        return pl.ds(wide * WIDE, WIDE)

    def owner_first(wide, d):
        return send(to_first.at[wide, peer(d)], block_in.at[0, r, :, columns(wide)],
                    owner_s.at[0], owner_r.at[wide], other(d))

    def owner_second(turn, d):
        return send(to_second.at[turn, peer(d)], block_in.at[1, r, :, pl.ds(turn * BACK, BACK)],
                    owner_s.at[1], owner_r.at[STEPS + turn], other(d))

    def route_first(wide):
        @pl.loop(0, REPS, unroll=4)
        def _(o):
            to_first[wide, o] = piece[wide, table[0, o * SLOTS]]

        @pl.loop(1, REPS)
        def _(d):
            owner_first(wide, d).start()

        block_in[0, r, :, columns(wide)] = to_first[wide, r]

    def route_second(turn):
        each = BACK // WIDE

        @pl.loop(0, REPS, unroll=4)
        def _(o):
            for i in range(each):
                to_second[turn, o, :, pl.ds(i * WIDE, WIDE)] = (
                    piece[turn * each + i, table[0, o * SLOTS + 1]])

        @pl.loop(1, REPS)
        def _(d):
            owner_second(turn, d).start()

        block_in[1, r, :, pl.ds(turn * BACK, BACK)] = to_second[turn, r]

    def wait_first(wide):
        landed(block_in.at[0, pl.ds(0, REPS - 1), :, columns(wide)], owner_r.at[wide])

    def wait_second(turn):
        landed(block_in.at[1, pl.ds(0, REPS - 1), :, pl.ds(turn * BACK, BACK)],
               owner_r.at[STEPS + turn])

    roots = [pltpu.make_async_copy(ref, root_in.at[i], root_sem.at[i])
             for i, ref in enumerate((left_root, right_root))]
    stats = [pltpu.make_async_copy(ref, stat_in.at[i], stat_sem.at[i])
             for i, ref in enumerate((left_stat, right_stat))]

    names = pltpu.make_async_copy(owner_list, owners, list_sem)

    start_far(0)
    names.start()
    start_near(0)
    start_far(1)
    for copy in roots:
        copy.start()

    names.wait()

    @pl.loop(0, REPS, unroll=4)
    def _(j):
        mine = owners[0, s * REPS + j]
        count = jnp.int32(0)
        for i in range(REPS):
            hit = (owners[0, s * REPS + i] == mine) & (i < j)
            count = count + hit.astype(jnp.int32)
        table[1, j] = mine
        table[2, j] = jnp.minimum(count, SLOTS - 1)

    @pl.loop(0, REPS, unroll=4)
    def _(o):
        first, second = jnp.int32(REPS), jnp.int32(REPS)
        for j in range(REPS):
            hit = table[1, j] == o
            first = jnp.where(hit & (table[2, j] == 0), j, first)
            second = jnp.where(hit & (table[2, j] == 1), j, second)
        table[0, o * SLOTS] = first
        table[0, o * SLOTS + 1] = second

    for wide in range(STEPS):
        piece[wide, REPS] = jnp.zeros((PIECE, WIDE), bf16)
    squares[...] = jnp.zeros_like(squares)

    def split(side):
        roots[side].wait()

        @pl.loop(0, SLOTS * 8)
        def _(i):
            k, t = i // 8, i % 8
            rows = pl.ds(pl.multiple_of(t * 64, 64), 64)
            whole = root_in[side, k, rows, :]
            top = whole.astype(bf16)
            root_hi[side, k, rows, :] = top
            root_lo[side, k, rows, :] = (whole - top.astype(f32)).astype(bf16)

    combine(0)
    start_near(1)
    start_far(2)
    start_far(3)
    for side in range(2):
        split(side)
    for wide in range(STEPS):
        if wide + 1 < STEPS:
            combine(wide + 1)
        if wide + 2 < STEPS:
            start_near(wide + 2)
        if wide >= 1 and not direct(wide):
            line_combine(wide - 1)
        line_total(wide)
        if direct(wide):
            line_combine(wide - 1)
        if wide == 0:
            for copy in stats:
                copy.start()
        if wide >= 1:
            total(wide - 1)
        if wide >= 2:
            route_first(wide - 2)
    route_first(STEPS - 2)
    route_second(0)
    total(STEPS - 1)
    route_first(STEPS - 1)

    def square(d):
        return send(squares_in.at[0], squares_in.at[d], square_s, square_r, other(d))

    squares_in[0] = jnp.sum(squares[...], axis=0, keepdims=True)

    @pl.loop(1, REPS)
    def _(d):
        square(d).start()

    route_second(1)


    def product(k, first, count):
        @pl.loop(0, 2)
        def _(t):
            rows = pl.ds(pl.multiple_of(t * 256, 256), 256)
            across = pl.ds(first, count)
            block = block_in[k, :, :, across].reshape(BLOCK, count)
            part = (jnp.dot(root_hi[0, k, rows, :], block, preferred_element_type=f32)
                    + jnp.dot(root_lo[0, k, rows, :], block, preferred_element_type=f32))
            top = part.astype(bf16)
            low = (part - top.astype(f32)).astype(bf16)
            hi, lo = root_hi[1, k, across, :], root_lo[1, k, across, :]
            value = (jnp.dot(top, hi, preferred_element_type=f32)
                     + jnp.dot(top, lo, preferred_element_type=f32)
                     + jnp.dot(low, hi, preferred_element_type=f32))
            if first > 0:
                value = precond[k, rows, :] + value
            precond[k, rows, :] = value
            if first + count == BLOCK:
                ready[k, pl.ds(t * 8, 8)] = value.astype(bf16).reshape(8, PIECE, BLOCK)

    def column_in_root():
        return send(column.at[0], column_in.at[s], column_s, column_r, (ROOT, r))

    def column_out(d):
        return send(column.at[1], column_in.at[ROOT], column_s, column_r, ((ROOT + d) % COLS, r))

    def hold_first(d):
        return send(ready.at[0, peer(d)], held_first.at[r], held_s.at[0], held_r.at[TURNS], other(d))

    def hold_second(turn, d):
        return send(ready.at[1, peer(d), :, pl.ds(turn * BACK, BACK)], held[turn].at[r],
                    held_s.at[1], held_r.at[turn], other(d))

    def start_second(turn):
        @pl.loop(1, REPS)
        def _(d):
            hold_second(turn, d).start()

        held[turn][r] = ready[1, r, :, pl.ds(turn * BACK, BACK)]

    def graft(k):
        def square_sum(i, carry):
            value, power = carry
            p = precond[k, pl.ds(pl.multiple_of(i * PIECE, PIECE), PIECE), :]
            g = block_in[k, i].astype(f32)
            return value + g * g, power + p * p

        zero = jnp.zeros((PIECE, BLOCK), f32)
        value, power = lax.fori_loop(0, REPS, square_sum, (zero, zero))
        value = jnp.sum(value, axis=(0, 1), keepdims=True) / (BLOCK * BLOCK)
        power = jnp.sum(power, axis=(0, 1), keepdims=True) / (BLOCK * BLOCK)
        scale = jnp.sqrt(value + epsilon) / jnp.sqrt(power + epsilon)
        scale_own[pl.ds(k, 1), :] = jnp.broadcast_to(scale, (1, 128))

    def scale_send(d):
        return send(scale_own, scale_in.at[r], scale_s, scale_r, other(d))

    wait_first(0)
    wait_first(1)
    product(0, 0, 2 * WIDE)
    wait_first(2)
    product(0, 2 * WIDE, WIDE)
    wait_first(3)
    landed(squares_in.at[pl.ds(1, REPS - 1)], square_r)
    column[0] = lax.fori_loop(1, REPS, lambda d, value: value + squares_in[d], squares_in[0])

    @pl.when(s != ROOT)
    def _():
        column_in_root().start()

    product(0, 3 * WIDE, WIDE)

    @pl.loop(1, REPS)
    def _(d):
        hold_first(d).start()

    held_first[r] = ready[0, r]
    wait_second(0)
    product(1, 0, BACK)
    wait_second(1)
    product(1, BACK, BACK)
    start_second(0)
    graft(0)
    graft(1)

    @pl.loop(1, REPS)
    def _(d):
        scale_send(d).start()

    scale_in[r] = scale_own[...]
    for turn in range(1, TURNS):
        start_second(turn)

    @pl.when(s == ROOT)
    def _():
        landed(column_in.at[pl.ds(0, COLS - 1)], column_r)

        def gather(d, value):
            return value + column_in[(ROOT + d) % COLS]

        column[1] = lax.fori_loop(1, COLS, gather, column[0])
        column_in[ROOT] = column[1]

        @pl.loop(1, COLS)
        def _(d):
            column_out(d).start()

    for copy in stats:
        copy.wait()

    @pl.loop(0, SLOTS)
    def _(k):
        filled = table[0, r * SLOTS + k] < REPS
        keep = jnp.where(filled, decay_keep, 1.0).astype(f32)
        weight = (1.0 - decay_keep) / BLOCK
        for t in range(2):
            rows = pl.ds(t * 256, 256)
            block = block_in[k].reshape(BLOCK, BLOCK)
            left = lax.dot_general(
                block[t * 256:(t + 1) * 256], block, (((1,), (1,)), ((), ())),
                preferred_element_type=f32)
            left_out[k, rows, :] = keep * stat_in[0, k, rows, :] + weight * left
            right = lax.dot_general(
                block[:, t * 256:(t + 1) * 256], block, (((0,), (0,)), ((), ())),
                preferred_element_type=f32)
            right_out[k, rows, :] = keep * stat_in[1, k, rows, :] + weight * right

    @pl.when(s != ROOT)
    def _():
        landed(column_in.at[ROOT], column_r)

    rms = jnp.sqrt(jnp.sum(column_in[ROOT], axis=(0, 1), keepdims=True)
                   / (COLS * REPS * BLOCK * BLOCK))
    clip = jnp.minimum(1.0, rms_limit / rms)

    landed(scale_in.at[pl.ds(0, REPS - 1)], scale_r)

    def settle(turn, d):
        return send(to_place.at[turn, peer(d)], update.at[r, :, pl.ds(turn * BACK, BACK)],
                    place_s, place_r, other(d))

    for turn in range(TURNS):
        if turn == 0:
            landed(held_first.at[pl.ds(0, REPS - 1)], held_r.at[TURNS])
        landed(held[turn].at[pl.ds(0, REPS - 1)], held_r.at[turn])

        @pl.loop(0, REPS, unroll=4)
        def _(j):
            o, k = table[1, j], table[2, j]
            scales = scale_in[o]
            scale = jnp.where(k == 0, scales[:1], scales[1:]) * clip
            value = jnp.where(k == 0, held_first[o, :, pl.ds(turn * BACK, BACK)], held[turn][o])
            value = value.astype(f32)
            for part in range(BACK // 128):
                to_place[turn, j, :, pl.ds(part * 128, 128)] = (
                    value[:, part * 128:(part + 1) * 128] * scale).astype(bf16)

        @pl.loop(1, REPS)
        def _(d):
            settle(turn, d).start()

        update[r, :, pl.ds(turn * BACK, BACK)] = to_place[turn, r]

    left(far_in, far_s)
    left(near_own, near_s)
    left(near_own, both_s)
    left(line_far, lfar_s)
    left(line_far, lnear_s)
    left(line_far, lboth_s)
    left(line_in, line_s)
    left(to_first.at[:, pl.ds(0, REPS - 1)], owner_s.at[0])
    left(to_second.at[:, pl.ds(0, REPS - 1)], owner_s.at[1])
    left(ready.at[0, pl.ds(0, REPS - 1)], held_s.at[0])
    left(ready.at[1, pl.ds(0, REPS - 1)], held_s.at[1])
    left(to_place.at[:, pl.ds(0, REPS - 1)], place_s)
    left(squares_in.at[pl.ds(1, REPS - 1)], square_s)
    left(scale_in.at[pl.ds(0, REPS - 1)], scale_s)

    @pl.when(s != ROOT)
    def _():
        left(column_in.at[ROOT], column_s)

    @pl.when(s == ROOT)
    def _():
        left(column_in.at[pl.ds(0, COLS - 1)], column_s)

    landed(update.at[pl.ds(0, REPS - 1)], place_r)


def on_device(partial_grads, owner_list, left_stat, right_stat, left_root, right_root):
    grads = partial_grads.reshape(REPS, SIDE, SIDE, 2, HALF, BLOCK)
    hbm_spec = pl.BlockSpec(memory_space=pltpu.HBM)
    vmem_spec = pl.BlockSpec(memory_space=pltpu.VMEM)
    dma = pltpu.SemaphoreType.DMA
    groups = 2 * STEPS
    lines = groups - 2
    quarter = (2, 8, SIDE, HALF, WIDE)
    eighth = (2, 8, HALF, WIDE)
    state = pltpu.VMEM((SLOTS, BLOCK, BLOCK), f32)
    update, left_new, right_new = pl.pallas_call(
        kernel,
        out_shape=(pltpu.VMEM((REPS, PIECE, BLOCK), bf16), state, state),
        in_specs=[hbm_spec] * 6,
        out_specs=(vmem_spec, vmem_spec, vmem_spec),
        scratch_shapes=[
            pltpu.VMEM((groups,) + quarter, bf16),
            pltpu.VMEM((groups, 2) + quarter, bf16),
            pltpu.VMEM((groups,) + quarter, bf16),
            pltpu.VMEM((groups, REPS, SIDE, HALF, WIDE), bf16),
            pltpu.VMEM((groups, SIDE, REPS, HALF, WIDE), bf16),
            pltpu.VMEM((lines,) + eighth, bf16),
            pltpu.VMEM((lines, 2) + eighth, bf16),
            pltpu.VMEM((2, 3, REPS, HALF, WIDE), bf16),
            pltpu.VMEM((STEPS, REPS + 1, PIECE, WIDE), bf16),
            pltpu.VMEM((STEPS, REPS, PIECE, WIDE), bf16),
            pltpu.VMEM((TURNS, REPS, PIECE, BACK), bf16),
            pltpu.VMEM((SLOTS, REPS, PIECE, BLOCK), bf16),
            pltpu.VMEM((2, SLOTS, BLOCK, BLOCK), f32),
            pltpu.VMEM((2, SLOTS, BLOCK, BLOCK), bf16),
            pltpu.VMEM((2, SLOTS, BLOCK, BLOCK), bf16),
            pltpu.VMEM((2, SLOTS, BLOCK, BLOCK), f32),
            pltpu.VMEM((SLOTS, BLOCK, BLOCK), f32),
            pltpu.VMEM((SLOTS, REPS, PIECE, BLOCK), bf16),
            pltpu.VMEM((REPS, PIECE, BLOCK), bf16),
            pltpu.VMEM((REPS, PIECE, BACK), bf16),
            pltpu.VMEM((REPS, PIECE, BACK), bf16),
            pltpu.VMEM((SLOTS, 128), f32),
            pltpu.VMEM((REPS, SLOTS, 128), f32),
            pltpu.VMEM((TURNS, REPS, PIECE, BACK), bf16),
            pltpu.VMEM((8, 128), f32),
            pltpu.VMEM((REPS, 1, 128), f32),
            pltpu.VMEM((2, 1, 128), f32),
            pltpu.VMEM((COLS, 1, 128), f32),
            pltpu.SMEM((1, COLS * REPS), jnp.int32),
            pltpu.SMEM((3, REPS * SLOTS), jnp.int32),
            dma((STEPS,)), dma((STEPS,)), dma((2,)), dma((2,)), dma,
            dma, dma((STEPS,)), dma, dma, dma((STEPS,)),
            dma, dma((STEPS - 1,)), dma, dma, dma((STEPS - 1,)),
            dma, dma, dma((2,)), dma((STEPS + TURNS,)),
            dma((2,)), dma((TURNS + 1,)), dma, dma, dma, dma,
            dma, dma, dma, dma,
        ],
        compiler_params=pltpu.CompilerParams(
            collective_id=0, has_side_effects=True, vmem_limit_bytes=58 << 20),
    )(grads, owner_list.reshape(1, COLS * REPS),
      left_stat[0, 0], right_stat[0, 0], left_root[0, 0], right_root[0, 0])
    return (update.reshape(1, BLOCK, BLOCK), left_new[None, None], right_new[None, None])


def solution(mesh):
    return jax.shard_map(
        on_device,
        mesh=mesh,
        in_specs=(
            P("replica", "shard", None, None),
            P(),
            P("shard", "replica", None, None, None),
            P("shard", "replica", None, None, None),
            P("shard", "replica", None, None, None),
            P("shard", "replica", None, None, None),
        ),
        out_specs=(
            P(("shard", "replica"), None, None),
            P("shard", "replica", None, None, None),
            P("shard", "replica", None, None, None),
        ),
        check_vma=False,
    )
```
